32 devices in a mesh: dp: 4 (over z), pack: 8 (over y, x, core).
Axes of the slice: x: 2, y: 2, z: 4, core: 2. Of those that a mesh axis runs over, the one named last changes fastest.
Arguments:
- enc_keys: bfloat16 [8192, 4096], P(('dp', 'pack')), may hold values from -4 to 4
- enc_values: bfloat16 [8192, 4096], P(('dp', 'pack')), may hold values from -6 to 6
- dec_queries: bfloat16 [4096, 4096], P(('dp', 'pack')), may hold values from -4 to 4
- cotangent: bfloat16 [4096, 4096], P(('dp', 'pack')), may hold values from -6 to 6
- input_lengths: int32 [4, 16], P('dp'), may hold values from 16 to 240, as said below
- target_lengths: int32 [4, 16], P('dp'), may hold values from 8 to 120, as said below
- enc_pack: int32 [4, 16], P('dp'), may hold values from 0 to 7, as said below
- dec_pack: int32 [4, 16], P('dp'), may hold values from 0 to 7, as said below
- task_group: int32 [4, 16, 1], P('dp'), may hold values from 0 to 15
- dro_weights: int32 [16], replicated, may hold values from 1 to 8
Outputs:
- queries_gradient: bfloat16 [4096, 4096], P(('dp', 'pack'))
- keys_gradient: bfloat16 [8192, 4096], P(('dp', 'pack'))
- values_gradient: bfloat16 [8192, 4096], P(('dp', 'pack'))
- group_loss: float32 [16], replicated
The draws below stay inside these ranges and needn't reach their ends.
Inputs may be any that keep to these rules, and one draw needn't show every extreme that they name: `input_lengths`: within one data group, the input lengths of the examples of one encoder pack add up to exactly 256; every length is a multiple of 16. `target_lengths`: within one data group, the target lengths of the examples of one decoder pack add up to exactly 128; every length is a multiple of 8. `enc_pack`: within one data group, every encoder pack holds exactly 2 examples. `dec_pack`: within one data group, every decoder pack holds exactly 2 examples.
All inputs are finite; a program needn't handle non-finite values.
Results may differ from the reference program's by a relative error of at most 0.012.
The reference program's roundings to bfloat16 on the way (of `attention_low`, `attended`, `upstream` and `scores_gradient`) count: a program that leaves them out, or rounds other values in their place, can miss the bound.
Values may be sent and summed in bfloat16 or wider, within the bound.
No kernel may reach another device: no remote copies, remote signals or barrier semaphores. Data moves between devices by JAX's collectives and lax.ppermute only.
A program may use at most 128 MiB of HBM per device.

```python
import jax
import jax.numpy as jnp
from jax import lax

HEADS = 64
HEAD_DIM = 64
D = 4096
ENC_DEV = 256
DEC_DEV = 128
EX_DEV = 2
GROUPS = 16
ENC_SLOT = 240
DEC_SLOT = 120
EX_GRP = 16
ENC_TOKENS = 8192
DEC_TOKENS = 4096
N_DP = 4
N_PACK = 8


def assignment(key, offset_salt):
    key = jax.random.fold_in(key, offset_salt)
    shuffled = jax.vmap(lambda one_key: jax.random.permutation(one_key, EX_DEV * N_PACK))(jax.random.split(key, N_DP))
    shuffled = shuffled.astype(jnp.int32)
    return (shuffled // EX_DEV, shuffled % EX_DEV)


def pack_pieces(key, per_pack, step_size):
    base = per_pack // EX_DEV
    reach = base // step_size - 1
    pair_count = EX_DEV // 2
    shifts = jax.random.randint(key, (N_DP, N_PACK, pair_count), -reach, reach + 1).astype(jnp.int32)
    forced_pack = jax.random.randint(jax.random.fold_in(key, 7), (N_DP, 1), 0, N_PACK)
    forced = (jnp.arange(N_PACK, dtype=jnp.int32)[None, :] == forced_pack)[:, :, None] & (jnp.arange(pair_count, dtype=jnp.int32)[None, None, :] == 0)
    shifts = jnp.where(forced, reach, shifts)
    longer = base + shifts * step_size
    shorter = base - shifts * step_size
    return jnp.stack([longer, shorter], axis=-1).reshape(N_DP, N_PACK, EX_DEV).astype(jnp.int32)


def lengths_for(pieces, pack_index, slot_index):
    flat_pieces = pieces.reshape(N_DP, N_PACK * EX_DEV)
    return jnp.take_along_axis(flat_pieces, pack_index * EX_DEV + slot_index, axis=1).astype(jnp.int32)


def draw_input_lengths(key, part):
    pack_index, slot_index = assignment(key, 11)
    key = jax.random.fold_in(key, 3)
    return lengths_for(pack_pieces(key, ENC_DEV, 16), pack_index, slot_index)


def draw_target_lengths(key, part):
    pack_index, slot_index = assignment(key, 21)
    key = jax.random.fold_in(key, 4)
    return lengths_for(pack_pieces(key, DEC_DEV, 8), pack_index, slot_index)


def draw_enc_pack(key, part):
    pack_index, slot_index = assignment(key, 11)
    return pack_index


def draw_dec_pack(key, part):
    pack_index, slot_index = assignment(key, 21)
    return pack_index


def draw_enc_keys(key, part):
    key = jax.random.fold_in(key, 5)
    row_total = ENC_DEV * N_PACK * N_DP
    sample = jnp.clip(0.35 * jax.random.normal(key, (row_total, D), jnp.float32), -4.0, 4.0)
    return jnp.clip(sample, -4.0, 4.0).astype(jnp.bfloat16)


def draw_dec_queries(key, part):
    key = jax.random.fold_in(key, 6)
    row_total = DEC_DEV * N_PACK * N_DP
    sample = jnp.clip(0.35 * jax.random.normal(key, (row_total, D), jnp.float32), -4.0, 4.0)
    return sample.astype(jnp.bfloat16)


def with_ends(values, stream_key, smallest, top_value):
    shape = values.shape
    place = [jax.random.randint(jax.random.fold_in(stream_key, axis), (), 0, shape[axis]) for axis in range(len(shape))]
    values = values.at[tuple(place)].set(smallest)
    longest = shape.index(max(shape))
    place[longest] = (place[longest] + 1) % shape[longest]
    return values.at[tuple(place)].set(top_value)


def level_of(rng, dims, cuts, least, high):
    loudness, own = 1.0, jax.random.fold_in(rng, 6)
    for axis_at, parts in cuts:
        steps = jnp.exp(jax.random.uniform(jax.random.fold_in(own, axis_at), (parts,), jnp.float32, least / len(cuts), high / len(cuts)))
        loudness = loudness * jnp.repeat(steps, dims[axis_at] // parts).reshape([-1 if axis == axis_at else 1 for axis in range(len(dims))])
    return loudness


def picks_of(own_key, rows, number_of, top, lift):
    order = jax.random.permutation(jax.random.fold_in(own_key, 1), number_of)
    boost = order
    for power in range(3):
        boost = boost * boost // number_of
    boost = boost * lift // number_of
    tickets = jax.random.randint(jax.random.fold_in(own_key, 2), (rows, number_of), 0, 4096) + boost
    fixed_rows = jax.random.permutation(jax.random.fold_in(own_key, 3), rows)[jnp.arange(number_of) % rows]
    tickets = jnp.where(jnp.arange(rows)[:, None] == fixed_rows[None, :], 1 << 14, tickets)
    merit = tickets * number_of + jnp.arange(number_of)
    return lax.top_k(merit.astype(jnp.int32), top)[1].astype(jnp.int32)


def bell_draw(rng, dims, width, limit, cuts=(), kind=jnp.bfloat16):
    loudness = level_of(rng, dims, cuts, -0.22, 0.18) if cuts else 1.0
    result = jax.random.normal(rng, dims, jnp.float32) * width * loudness
    return jnp.minimum(jnp.maximum(result, -limit), limit).astype(kind)


def setup_inputs(seed: int = 0) -> dict:
    arg_keys = jax.random.split(jax.random.key(seed), 11)
    enc_keys = draw_enc_keys(jax.random.fold_in(arg_keys[10], 71), 0)
    enc_values = bell_draw(arg_keys[1], (ENC_TOKENS, D), 1.0, 6.0, ((0, 32),))
    dec_queries = draw_dec_queries(jax.random.fold_in(arg_keys[10], 71), 0)
    cotangent = bell_draw(arg_keys[3], (DEC_TOKENS, D), 1.0, 6.0, ((0, 32),))
    input_lengths = draw_input_lengths(jax.random.fold_in(arg_keys[10], 71), 0)
    target_lengths = draw_target_lengths(jax.random.fold_in(arg_keys[10], 71), 0)
    enc_pack = draw_enc_pack(jax.random.fold_in(arg_keys[10], 71), 0)
    dec_pack = draw_dec_pack(jax.random.fold_in(arg_keys[10], 71), 0)
    task_group = picks_of(arg_keys[8], N_DP * EX_GRP, GROUPS, 1, 1024).reshape((N_DP, EX_GRP, 1))
    dro_weights = with_ends(jax.random.randint(arg_keys[9], (GROUPS,), 1, 9), jax.random.fold_in(arg_keys[9], 1), 1, 8).astype(jnp.int32)
    return {"enc_keys": enc_keys, "enc_values": enc_values, "dec_queries": dec_queries, "cotangent": cotangent, "input_lengths": input_lengths, "target_lengths": target_lengths, "enc_pack": enc_pack, "dec_pack": dec_pack, "task_group": task_group, "dro_weights": dro_weights}


def owner_value(member, values):
    return jnp.sum(jnp.where(member, values[:, None], 0), axis=0).astype(values.dtype)


def pack_tables(lengths, pack_index, per_pack, slot_total, pack_total):
    ordinal = jnp.arange(lengths.shape[0], dtype=jnp.int32)
    same_pack = pack_index[:, None] == pack_index[None, :]
    earlier = ordinal[None, :] < ordinal[:, None]
    offsets = jnp.sum(jnp.where(same_pack & earlier, lengths[None, :], 0), axis=1).astype(jnp.int32)
    places = jnp.arange(slot_total, dtype=jnp.int32)
    inside = places[None, :] < lengths[:, None]
    starts = pack_index * per_pack + offsets
    gather_rows = (starts[:, None] + jnp.minimum(places[None, :], lengths[:, None] - 1)).astype(jnp.int32)
    tokens = jnp.arange(pack_total * per_pack, dtype=jnp.int32)
    token_pack = tokens // per_pack
    token_place = tokens % per_pack
    member = (pack_index[:, None] == token_pack[None, :]) & (offsets[:, None] <= token_place[None, :]) & (token_place[None, :] < (offsets + lengths)[:, None])
    owners = owner_value(member, ordinal)
    flat_slot = (owners * slot_total + token_place - owner_value(member, offsets)).astype(jnp.int32)
    return gather_rows, inside, member, flat_slot


def probabilities(query_split, key_split, key_inside):
    scores = jnp.einsum("qhd,khd->hqk", query_split, key_split)
    scores = jnp.where(key_inside[None, None, :], scores, -1e30)
    highest = jnp.max(scores, axis=-1, keepdims=True)
    powers = jnp.exp(scores - highest)
    return powers / jnp.sum(powers, axis=-1, keepdims=True)


def example_terms(query_rows, key_rows, value_rows, gradient, cotangent_rows, key_inside):
    query_slots = query_rows.shape[0]
    key_slots = key_rows.shape[0]
    query_split = query_rows.astype(jnp.float32).reshape(query_slots, HEADS, HEAD_DIM)
    key_split = key_rows.astype(jnp.float32).reshape(key_slots, HEADS, HEAD_DIM)
    value_split = value_rows.astype(jnp.float32).reshape(key_slots, HEADS, HEAD_DIM)
    gradient_split = gradient.astype(jnp.float32).reshape(query_slots, HEADS, HEAD_DIM)
    attention = probabilities(query_split, key_split, key_inside)
    attention_low = lax.optimization_barrier(attention.astype(jnp.bfloat16)).astype(jnp.float32)
    attended = jnp.einsum("hqk,khd->qhd", attention_low, value_split).astype(jnp.bfloat16)
    attended_split = lax.optimization_barrier(attended).astype(jnp.float32)
    token_loss = jnp.sum(attended_split.reshape(query_slots, -1) * cotangent_rows.astype(jnp.float32), axis=1)
    value_gradient = jnp.einsum("hqk,qhd->khd", attention_low, gradient_split).astype(jnp.bfloat16)
    attention_gradient = jnp.einsum("qhd,khd->hqk", gradient_split, value_split)
    row_drift = jnp.einsum("qhd,qhd->hq", gradient_split, attended_split)
    scores_gradient = (attention * (attention_gradient - row_drift[:, :, None])).astype(jnp.bfloat16)
    scores_gradient = lax.optimization_barrier(scores_gradient).astype(jnp.float32)
    query_gradient = jnp.einsum("hqk,khd->qhd", scores_gradient, key_split).astype(jnp.bfloat16)
    key_gradient = jnp.einsum("hqk,qhd->khd", scores_gradient, query_split).astype(jnp.bfloat16)
    return query_gradient.reshape(query_slots, -1), key_gradient.reshape(key_slots, -1), value_gradient.reshape(key_slots, -1), token_loss


def reference(enc_keys, enc_values, dec_queries, cotangent, input_lengths, target_lengths, enc_pack, dec_pack, task_group, dro_weights):
    group_index = jnp.arange(GROUPS, dtype=jnp.int32)
    task_ids = task_group[:, :, 0]
    counts = jnp.sum(jnp.where(task_ids[:, :, None] == group_index, target_lengths[:, :, None], 0), axis=(0, 1)).astype(jnp.float32)
    weights = dro_weights.astype(jnp.float32)
    scales = weights / jnp.sum(weights) * (DEC_TOKENS / counts)

    def one_group(entries):
        key_table, value_table, query_table, cotangent_rows, encoder_lengths, decoder_lengths, encoder_packs, decoder_packs, task_row = entries
        key_rows, key_inside, key_member, key_flat = pack_tables(encoder_lengths, encoder_packs, ENC_DEV, ENC_SLOT, N_PACK)
        query_rows, query_inside, query_member, query_flat = pack_tables(decoder_lengths, decoder_packs, DEC_DEV, DEC_SLOT, N_PACK)
        example_scale = jnp.sum(jnp.where(task_row[:, None] == group_index[None, :], scales[None, :], 0.0), axis=1)
        token_scale = owner_value(query_member, example_scale)
        token_group = owner_value(query_member, task_row)
        upstream = (cotangent_rows.astype(jnp.float32) * token_scale[:, None]).astype(jnp.bfloat16)

        def one_example(items):
            rows_query, rows_key, inside_key, inside_query = items
            gradient = jnp.where(inside_query[:, None], upstream[rows_query], jnp.zeros((), jnp.bfloat16))
            return example_terms(query_table[rows_query], key_table[rows_key], value_table[rows_key], gradient, cotangent_rows[rows_query], inside_key)

        query_padded, key_padded, value_padded, loss_padded = lax.map(one_example, (query_rows, key_rows, key_inside, query_inside))
        feature_width = query_table.shape[1]
        queries_result = query_padded.reshape(-1, feature_width)[query_flat]
        keys_result = key_padded.reshape(-1, feature_width)[key_flat]
        values_result = value_padded.reshape(-1, feature_width)[key_flat]
        token_loss = loss_padded.reshape(-1)[query_flat]
        partial_value = jnp.sum(jnp.where(token_group[None, :] == group_index[:, None], token_loss[None, :], 0.0), axis=1)
        return queries_result, keys_result, values_result, partial_value

    stacked = (enc_keys.reshape(N_DP, -1, D), enc_values.reshape(N_DP, -1, D), dec_queries.reshape(N_DP, -1, D), cotangent.reshape(N_DP, -1, D), input_lengths, target_lengths, enc_pack, dec_pack, task_ids)
    queries_gradient, keys_gradient, values_gradient, partials = lax.map(one_group, stacked)
    group_loss = jnp.sum(partials, axis=0) / counts
    return queries_gradient.reshape(-1, D), keys_gradient.reshape(-1, D), values_gradient.reshape(-1, D), group_loss
```

```python
import functools

import jax
import jax.numpy as jnp
from jax import lax
from jax.experimental import pallas as pl
from jax.experimental.pallas import tpu as pltpu
from jax.sharding import PartitionSpec as P

HEAD_DIM = 64
PAIR = 2 * HEAD_DIM
EX_DEV = 2
GROUPS = 16
CHUNKS = 4
UNROLL = 2
ALONE = pltpu.CompilerParams(vmem_limit_bytes=60 * 1024 * 1024)
ROOM = pltpu.CompilerParams(vmem_limit_bytes=16 * 1024 * 1024)
FIELDS = 8
SMALL = pl.CostEstimate(flops=0, bytes_accessed=2 * 1024 * 1024, transcendentals=0)
ANY = pl.BlockSpec(memory_space=pl.ANY)
HBM = pl.BlockSpec(memory_space=pltpu.HBM)
SMEM = pl.BlockSpec(memory_space=pltpu.SMEM)
VMEM = pl.BlockSpec(memory_space=pltpu.VMEM)


def table_kernel(
    me_ref,
    input_ref,
    target_ref,
    enc_ref,
    dec_ref,
    task_ref,
    k_ref,
    v_ref,
    *refs,
):
    kv_ref, table_ref, count_ref, held, sem = refs[-5:]
    me = me_ref[0]
    core = lax.rem(me, 2)
    half = held.shape[-1]
    columns = pl.ds(pl.multiple_of((1 - core) * half, half), half)
    into = [
        pltpu.make_async_copy(source.at[:, columns], held.at[tensor], sem.at[tensor])
        for tensor, source in enumerate((k_ref, v_ref))
    ]
    out = [
        pltpu.make_async_copy(held.at[tensor], kv_ref.at[tensor], sem.at[2 + tensor])
        for tensor in range(2)
    ]
    for copy in into:
        copy.start()
    total = enc_ref.shape[1]
    for side in range(2):
        pack = me + side * (1 - 2 * core)

        def find(item, carry, pack=pack):
            first, second = carry
            hit = enc_ref[0, item] == pack
            return (
                jnp.where(hit & (first < 0), item, first),
                jnp.where(hit & (first >= 0), item, second),
            )

        first, second = lax.fori_loop(0, total, find, (jnp.int32(-1), jnp.int32(-1)))
        second = jnp.maximum(second, 0)
        first = jnp.maximum(first, 0)
        for place, item in enumerate((first, second)):
            row = 2 * side + place
            dec = dec_ref[0, item]

            def before(other, offset, dec=dec):
                return offset + jnp.where(dec_ref[0, other] == dec, target_ref[0, other], 0)

            table_ref[row, 0] = dec ^ me
            table_ref[row, 1] = lax.fori_loop(0, item, before, jnp.int32(0))
            table_ref[row, 2] = target_ref[0, item]
            table_ref[row, 3] = jnp.int32(0) if place == 0 else input_ref[0, first]
            table_ref[row, 4] = input_ref[0, item]
            table_ref[row, 5] = task_ref[0, item]
            table_ref[row, 6] = 0
            table_ref[row, 7] = 0
    lane = lax.broadcasted_iota(jnp.int32, (1, 128), 1)
    counts = jnp.zeros((1, 128), jnp.float32)
    for item in range(total):
        amount = target_ref[0, item].astype(jnp.float32)
        counts = counts + jnp.where(lane == task_ref[0, item], amount, 0.0)
    count_ref[...] = counts
    for tensor in range(2):
        into[tensor].wait()
        out[tensor].start()
    for tensor in range(2):
        out[tensor].wait()


def tabulate(me, lengths, targets, enc_pack, dec_pack, task, keys, values, waits):
    rows, features = keys.shape
    half = features // 2
    return pl.pallas_call(
        table_kernel,
        out_shape=[
            jax.ShapeDtypeStruct((2, rows, half), keys.dtype),
            jax.ShapeDtypeStruct((4, FIELDS), jnp.int32),
            jax.ShapeDtypeStruct((1, 128), jnp.float32),
        ],
        in_specs=[SMEM] * 6 + [HBM] * 2 + [ANY] * len(waits),
        out_specs=[ANY, SMEM, VMEM],
        scratch_shapes=[pltpu.VMEM((2, rows, half), keys.dtype), pltpu.SemaphoreType.DMA((4,))],
        compiler_params=ROOM,
        cost_estimate=SMALL,
        name="tabulate",
    )(me, lengths, targets, enc_pack, dec_pack, task, keys, values, *waits)


def split_kernel(me_ref, q_ref, c_ref, own_ref, other_ref, held, sem):
    half = held.shape[-1]
    core = lax.rem(me_ref[0], 2)
    into, out = [], []
    for side, (base, target) in enumerate(((core, own_ref), (1 - core, other_ref))):
        columns = pl.ds(pl.multiple_of(base * half, PAIR), half)
        for tensor, source in enumerate((q_ref, c_ref)):
            place = 2 * side + tensor
            into.append(
                pltpu.make_async_copy(source.at[:, columns], held.at[place], sem.at[place])
            )
            out.append(
                pltpu.make_async_copy(held.at[place], target.at[tensor], sem.at[4 + place])
            )
    for copy in into:
        copy.start()
    for place in range(4):
        into[place].wait()
        out[place].start()
    for copy in out:
        copy.wait()


def split(me, queries, cotangent):
    rows, features = queries.shape
    half = features // 2
    return pl.pallas_call(
        split_kernel,
        out_shape=[jax.ShapeDtypeStruct((2, rows, half), queries.dtype)] * 2,
        in_specs=[SMEM] + [HBM] * 2,
        out_specs=[ANY] * 2,
        scratch_shapes=[
            pltpu.VMEM((4, rows, half), queries.dtype),
            pltpu.SemaphoreType.DMA((8,)),
        ],
        compiler_params=ROOM,
        cost_estimate=SMALL,
        name="split_columns",
    )(me, queries, cotangent)


def layout(packs):
    if packs == 8:
        return [(0, 2), (2, 2), (4, 2), (6, 1), (7, 1)]
    return [(first, 2) for first in range(0, packs, 2)]


def attention_kernel(
    me_ref, table_ref, scale_ref, *refs, packs, first, waits, half, at
):
    places = layout(packs)
    sources = len(places)
    pieces = refs[:packs]
    k_ref, v_ref, sibling_ref = refs[packs : packs + 3]
    outs = refs[packs + 3 + (0 if first else 3) + waits :]
    k_out, v_out, sibling_out = outs[:3]
    query_outs = outs[3 : 3 + sources]
    loss_out = outs[3 + sources]
    kv, qc, dq, dkv, loss, bias, scaling, in_sem, qc_sem, out_sem, dkv_sem = outs[sources + 4 :]
    width = qc.shape[-1]
    rows = qc.shape[2]
    keys = kv.shape[2]
    core = lax.rem(me_ref[0], 2)
    own_columns = pl.ds(pl.multiple_of(core * half + at, PAIR), width)
    half_columns = pl.ds(at, width)
    kv_copies = [
        [
            pltpu.make_async_copy(k_ref.at[:, own_columns], kv.at[0, 0], in_sem.at[0, 0]),
            pltpu.make_async_copy(v_ref.at[:, own_columns], kv.at[0, 1], in_sem.at[0, 1]),
        ],
        [
            pltpu.make_async_copy(
                sibling_ref.at[tensor, :, half_columns], kv.at[1, tensor], in_sem.at[1, tensor]
            )
            for tensor in range(2)
        ],
    ]
    dkv_copies = [
        [
            pltpu.make_async_copy(dkv.at[0, 0], k_out.at[:, own_columns], dkv_sem.at[0, 0]),
            pltpu.make_async_copy(dkv.at[0, 1], v_out.at[:, own_columns], dkv_sem.at[0, 1]),
        ],
        [
            pltpu.make_async_copy(
                dkv.at[1, tensor], sibling_out.at[tensor, :, half_columns], dkv_sem.at[1, tensor]
            )
            for tensor in range(2)
        ],
    ]
    for side in range(2):
        for copy in kv_copies[side]:
            copy.start()
        for place in range(2):
            item = 2 * side + place
            owner = table_ref[item, 0]
            for distance, piece in enumerate(pieces):

                @pl.when(owner == distance)
                def _(piece=piece, item=item):
                    pltpu.make_async_copy(
                        piece.at[:, :, half_columns], qc.at[item], qc_sem.at[item]
                    ).start()

    dq[...] = jnp.zeros_like(dq)
    loss[...] = jnp.zeros_like(loss)
    lane = lax.broadcasted_iota(jnp.int32, (1, PAIR), 1)
    low = lane < HEAD_DIM
    row = lax.broadcasted_iota(jnp.int32, (rows, PAIR), 0)
    row_lane = lax.broadcasted_iota(jnp.int32, (1, rows), 1)
    key = lax.broadcasted_iota(jnp.int32, (keys, rows), 0)

    def dot(left, right):
        return jnp.dot(left, right, preferred_element_type=jnp.float32)

    vector = jnp.zeros((1, 128), jnp.float32)
    for side in range(2):
        for copy in kv_copies[side]:
            copy.wait()
        for place in range(2):
            item = 2 * side + place
            pltpu.make_async_copy(
                pieces[0].at[:, :, half_columns], qc.at[item], qc_sem.at[item]
            ).wait()
        owner, scale_rows = [], []
        for place in range(2):
            item = 2 * side + place
            start, length = table_ref[item, 1], table_ref[item, 2]
            key_start, key_length = table_ref[item, 3], table_ref[item, 4]
            scale = scale_ref[0, table_ref[item, 5]]
            span = slice(place * rows, (place + 1) * rows)
            bias[:, span] = jnp.where(
                (key >= key_start) & (key < key_start + key_length), 0.0, -1e30
            )
            scaling[span] = jnp.where((row >= start) & (row < start + length), scale, 0.0)
            scale_rows.append(
                jnp.where((row_lane >= start) & (row_lane < start + length), scale, 0.0)
            )
            owner.append(table_ref[item, 0])
        scale_row = jnp.concatenate(scale_rows, axis=1)

        def pair_step(pair, carry, side=side, owner=owner, scale_row=scale_row):
            columns = pl.ds(pl.multiple_of(pair * PAIR, PAIR), PAIR)
            key_pair = kv[side, 0, :, columns]
            value_pair = kv[side, 1, :, columns]
            query = jnp.concatenate([qc[2 * side + place, 0, :, columns] for place in range(2)], axis=0)
            cot = jnp.concatenate([qc[2 * side + place, 1, :, columns] for place in range(2)], axis=0)
            zero = jnp.zeros_like(key_pair)

            def heads(array):
                return jnp.concatenate(
                    [jnp.where(low, array, zero), jnp.where(low, zero, array)], axis=0
                )

            up = (cot.astype(jnp.float32) * scaling[...]).astype(jnp.bfloat16)
            query_turned, key_turned, value_turned = query.T, key_pair.T, value_pair.T
            cot_turned = cot.T.astype(jnp.float32)
            up_turned = (cot_turned * scale_row).astype(jnp.bfloat16)
            both_scores = dot(heads(key_pair), query_turned)
            both_slopes = dot(heads(value_pair), up_turned)
            query_parts, weights_parts, grad_parts = [], [], []
            for head in range(2):
                spread = slice(head * keys, (head + 1) * keys)
                part = slice(head * HEAD_DIM, (head + 1) * HEAD_DIM)
                scores = both_scores[spread] + bias[...]
                highest = jnp.max(scores, axis=0, keepdims=True)
                powers = jnp.exp(scores - highest)
                weights = powers * (1.0 / jnp.sum(powers, axis=0, keepdims=True))
                weights_low = weights.astype(jnp.bfloat16)
                attended = dot(value_turned[part], weights_low)
                attended = attended.astype(jnp.bfloat16).astype(jnp.float32)
                token = cot_turned[part] * attended
                loss[side] += jnp.sum(token.reshape(HEAD_DIM // 8, 8, 2 * rows), axis=0)
                drift = jnp.sum(
                    up_turned[part].astype(jnp.float32) * attended, axis=0, keepdims=True
                )
                grad = (weights * (both_slopes[spread] - drift)).astype(jnp.bfloat16)
                query_parts.append(dot(key_turned[part], grad))
                grad_parts.append(grad)
                weights_parts.append(weights_low)
            query_grad = jnp.concatenate(query_parts, axis=0).astype(jnp.bfloat16).T
            for place in range(2):
                at = owner[place]
                span = slice(place * rows, (place + 1) * rows)
                dq[at, :, columns] = dq[at, :, columns] + query_grad[span]
            key_grad = dot(jnp.concatenate(grad_parts, axis=1), heads(query))
            value_grad = dot(jnp.concatenate(weights_parts, axis=1), heads(up))
            dkv[side, 0, :, columns] = key_grad.astype(jnp.bfloat16)
            dkv[side, 1, :, columns] = value_grad.astype(jnp.bfloat16)
            return carry

        lax.fori_loop(0, width // PAIR, pair_step, 0, unroll=UNROLL)
        for copy in dkv_copies[side]:
            copy.start()
        for place in range(2):
            item = 2 * side + place
            start, length = table_ref[item, 1], table_ref[item, 2]
            part = jnp.sum(loss[side][:, place * rows : (place + 1) * rows], axis=0, keepdims=True)
            part = jnp.where((row_lane >= start) & (row_lane < start + length), part, 0.0)
            amount = jnp.sum(part, axis=1, keepdims=True)
            vector = vector + jnp.where(lane == table_ref[item, 5], amount, 0.0)

    query_copies = [
        pltpu.make_async_copy(
            dq.at[pl.ds(base, 2)] if count == 2 else dq.at[base], target, out_sem.at[i]
        )
        for i, (target, (base, count)) in enumerate(zip(query_outs, places))
    ]
    for copy in query_copies:
        copy.start()
    loss_out[...] = vector
    for side in range(2):
        for copy in dkv_copies[side]:
            copy.wait()
    for copy in query_copies:
        copy.wait()


def attention_chunk(
    me, table, scales, pieces, keys, values, sibling, full, waits, packs, at, width
):
    sources = len(layout(packs))
    rows = pieces[0].shape[1]
    key_rows, features = keys.shape
    half = features // 2
    low = jnp.bfloat16
    first = full is None
    flops = rows * key_rows * width
    before = 3 + packs + 3
    return pl.pallas_call(
        functools.partial(
            attention_kernel,
            packs=packs,
            first=first,
            waits=len(waits),
            half=half,
            at=at,
        ),
        out_shape=[
            jax.ShapeDtypeStruct(keys.shape, low),
            jax.ShapeDtypeStruct(keys.shape, low),
            jax.ShapeDtypeStruct((2, key_rows, half), low),
        ]
        + [
            jax.ShapeDtypeStruct((count, rows, width)[2 - count :], low)
            for _, count in layout(packs)
        ]
        + [jax.ShapeDtypeStruct((1, 128), jnp.float32)],
        in_specs=[SMEM] * 3 + [ANY] * packs + [HBM] * 2 + [ANY] + [HBM] * (0 if first else 3) + [ANY] * len(waits),
        out_specs=[HBM] * 3 + [ANY] * sources + [VMEM],
        scratch_shapes=[
            pltpu.VMEM((2, 2, key_rows, width), low),
            pltpu.VMEM((4, 2, rows, width), low),
            pltpu.VMEM((packs, rows, width), low),
            pltpu.VMEM((2, 2, key_rows, width), low),
            pltpu.VMEM((2, 8, 2 * rows), jnp.float32),
            pltpu.VMEM((key_rows, 2 * rows), jnp.float32),
            pltpu.VMEM((2 * rows, PAIR), jnp.float32),
            pltpu.SemaphoreType.DMA((2, 2)),
            pltpu.SemaphoreType.DMA((4,)),
            pltpu.SemaphoreType.DMA((sources,)),
            pltpu.SemaphoreType.DMA((2, 2)),
        ],
        input_output_aliases={} if first else {before + i: i for i in range(3)},
        compiler_params=ROOM,
        cost_estimate=pl.CostEstimate(
            flops=flops, bytes_accessed=8 * 1024 * 1024, transcendentals=0
        ),
        name="attention_chunk",
    )(me, table, scales, *pieces, keys, values, sibling, *(() if first else full), *waits)


def finish_kernel(me_ref, *refs, spots, half, with_keys):
    count = 2 * len(spots)
    outs = refs[-1 - (3 if with_keys else 1) : -1]
    sem = refs[-1]
    core = lax.rem(me_ref[0], 2)
    moves = []
    for i, (at, width) in enumerate(spots):
        for side, base in enumerate((core, 1 - core)):
            columns = pl.ds(pl.multiple_of(base * half + at, PAIR), width)
            moves.append((refs[2 * i + side], outs[0], columns))
    if with_keys:
        other = pl.ds(pl.multiple_of((1 - core) * half, PAIR), half)
        moves += [(refs[count].at[tensor], outs[1 + tensor], other) for tensor in range(2)]
    copies = [
        pltpu.make_async_copy(source, out.at[:, columns], sem.at[i])
        for i, (source, out, columns) in enumerate(moves)
    ]
    for copy in copies:
        copy.start()
    for copy in copies:
        copy.wait()


def finish(me, parts, spots, like, back=None, given=()):
    with_keys = back is not None
    read = len(parts) + (1 if with_keys else 0)
    shapes = [jax.ShapeDtypeStruct(like.shape, like.dtype)]
    if with_keys:
        shapes += [jax.ShapeDtypeStruct(array.shape, array.dtype) for array in given]
    skipped = len(shapes) - len(given)
    return pl.pallas_call(
        functools.partial(
            finish_kernel, spots=spots, half=like.shape[1] // 2, with_keys=with_keys
        ),
        out_shape=shapes,
        in_specs=[SMEM] + [VMEM] * read + [HBM] * len(given),
        out_specs=[HBM] * len(shapes),
        scratch_shapes=[pltpu.SemaphoreType.DMA((len(parts) + 2,))],
        input_output_aliases={1 + read + i: skipped + i for i in range(len(given))},
        compiler_params=ROOM,
        cost_estimate=SMALL,
        name="finish",
    )(me, *parts, *((back,) if with_keys else ()), *given)


def swap(array, axis_name, size, bits):
    return lax.ppermute(array, axis_name, [(i, i ^ bits) for i in range(size)])


def after(vector, arrays):
    for array in arrays:
        vector = vector + 0.0 * array[0, 0, 0].astype(jnp.float32)
    return vector


def group_sum(array, axis_name, size):
    step = 1
    while step < size:
        if 4 * step <= size:
            first, second, third = (swap(array, axis_name, size, step * i) for i in (1, 2, 3))
            array = (array + first) + (second + third)
            step *= 4
        else:
            array = array + swap(array, axis_name, size, step)
            step *= 2
    return array


def local(
    enc_keys,
    enc_values,
    dec_queries,
    cotangent,
    input_lengths,
    target_lengths,
    enc_pack,
    dec_pack,
    task_group,
    dro_weights,
    *,
    packs,
    groups,
):
    me = lax.axis_index("pack").astype(jnp.int32).reshape(1)
    rows, features = dec_queries.shape
    half = features // 2
    total_tokens = rows * packs * groups
    relayed = packs == 8

    def swapped(array, bits):
        return swap(array, "pack", packs, bits)

    own, other = split(me, dec_queries, cotangent)
    pieces = [own]
    for bits in range(1, 6 if relayed else packs):
        pieces.append(swapped(other if bits & 1 else own, bits))
    if relayed:
        pieces += [swapped(pieces[2], 4), swapped(pieces[5], 2)]
    kv_other, table, group_counts = tabulate(
        me,
        input_lengths,
        target_lengths,
        enc_pack,
        dec_pack,
        task_group[:, :, 0],
        enc_keys,
        enc_values,
        [own],
    )
    kv_sibling = swapped(kv_other, 1)
    counts = group_sum(group_counts, "dp", groups)
    weights = dro_weights.astype(jnp.float32)
    weights = jnp.pad(weights, (0, 128 - GROUPS)).reshape(1, 128)
    scales = weights / jnp.sum(weights) * (total_tokens / counts)

    full, losses, query_parts, spots = None, [], [], []
    halfway, whole = [], []
    width = half // CHUNKS
    for chunk in range(CHUNKS):
        at = chunk * width
        order = sum(halfway[:-1][-1:], []) + whole[:-2][-1:]
        *result, loss = attention_chunk(
            me, table, scales, pieces, enc_keys, enc_values, kv_sibling, full,
            order, packs, at, width,
        )
        full, parts = result[:3], result[3:]
        losses.append(loss)
        if relayed:
            far = swapped(parts.pop(), 4)
            near = swapped(parts.pop(), 2)
            parts[2] = parts[2] + jnp.stack([near, jnp.zeros_like(near)])
            parts[1] = parts[1] + jnp.stack([jnp.zeros_like(far), far])
            halfway.append(parts[1:])
        summed = parts[0]
        for chip in range(1, len(parts)):
            summed = summed + swapped(parts[chip], 2 * chip)
        whole.append(summed)
        query_parts += [summed[0], swapped(summed[1], 1)]
        spots.append((at, width))
    back = swapped(full[2], 1)
    queries_gradient, keys_gradient, values_gradient = finish(
        me, query_parts[:-2], spots[:-1], dec_queries, back, full[:2]
    )
    (queries_gradient,) = finish(
        me, query_parts[-2:], spots[-1:], dec_queries, None, (queries_gradient,)
    )
    loss = functools.reduce(jnp.add, losses)
    loss = group_sum(after(loss, whole[-3:-2]), "pack", packs)
    loss = group_sum(after(loss, parts[1:]), "dp", groups)
    group_loss = (loss / counts)[0, :GROUPS]
    return (queries_gradient, keys_gradient, values_gradient, group_loss)


def solution(mesh):
    placed = (
        P(("dp", "pack"), None),
        P(("dp", "pack"), None),
        P(("dp", "pack"), None),
        P(("dp", "pack"), None),
        P("dp", None),
        P("dp", None),
        P("dp", None),
        P("dp", None),
        P("dp", None, None),
        P(),
    )
    return jax.shard_map(
        functools.partial(local, packs=mesh.shape["pack"], groups=mesh.shape["dp"]),
        mesh=mesh,
        in_specs=placed,
        out_specs=(P(("dp", "pack"), None), P(("dp", "pack"), None), P(("dp", "pack"), None), P()),
        check_vma=False,
    )
```

```python
import functools
import itertools
import math

import jax
import jax.numpy as jnp
from jax import lax
from jax.experimental import pallas as pl
from jax.experimental.pallas import tpu as pltpu
from jax.sharding import PartitionSpec as P

HEAD_DIM = 64
PAIR = 2 * HEAD_DIM
EX_DEV = 2
GROUPS = 16
CHUNKS = (1, 1)
LOCKSTEP = 4
ALONE = pltpu.CompilerParams(vmem_limit_bytes=60 * 1024 * 1024)
ROOM = pltpu.CompilerParams(vmem_limit_bytes=16 * 1024 * 1024)
FIELDS = 8
SMALL = pl.CostEstimate(flops=0, bytes_accessed=2 * 1024 * 1024, transcendentals=0)
ANY = pl.BlockSpec(memory_space=pl.ANY)
HBM = pl.BlockSpec(memory_space=pltpu.HBM)
SMEM = pl.BlockSpec(memory_space=pltpu.SMEM)
VMEM = pl.BlockSpec(memory_space=pltpu.VMEM)


def table_kernel(
    me_ref,
    input_ref,
    target_ref,
    enc_ref,
    dec_ref,
    task_ref,
    k_ref,
    v_ref,
    *refs,
):
    kv_ref, table_ref, count_ref, held, sem = refs[-5:]
    me = me_ref[0]
    core = lax.rem(me, 2)
    half = held.shape[-1]
    columns = pl.ds(pl.multiple_of((1 - core) * half, half), half)
    into = [
        pltpu.make_async_copy(source.at[:, columns], held.at[tensor], sem.at[tensor])
        for tensor, source in enumerate((k_ref, v_ref))
    ]
    out = [
        pltpu.make_async_copy(held.at[tensor], kv_ref.at[tensor], sem.at[2 + tensor])
        for tensor in range(2)
    ]
    for copy in into:
        copy.start()
    total = enc_ref.shape[1]
    for side in range(2):
        pack = me + side * (1 - 2 * core)

        def find(item, carry, pack=pack):
            first, second = carry
            hit = enc_ref[0, item] == pack
            return (
                jnp.where(hit & (first < 0), item, first),
                jnp.where(hit & (first >= 0), item, second),
            )

        first, second = lax.fori_loop(0, total, find, (jnp.int32(-1), jnp.int32(-1)))
        second = jnp.maximum(second, 0)
        first = jnp.maximum(first, 0)
        for place, item in enumerate((first, second)):
            row = 2 * side + place
            dec = dec_ref[0, item]

            def before(other, offset, dec=dec):
                return offset + jnp.where(dec_ref[0, other] == dec, target_ref[0, other], 0)

            table_ref[row, 0] = dec ^ me
            table_ref[row, 1] = lax.fori_loop(0, item, before, jnp.int32(0))
            table_ref[row, 2] = target_ref[0, item]
            table_ref[row, 3] = jnp.int32(0) if place == 0 else input_ref[0, first]
            table_ref[row, 4] = input_ref[0, item]
            table_ref[row, 5] = task_ref[0, item]
            table_ref[row, 6] = 0
            table_ref[row, 7] = 0
    lane = lax.broadcasted_iota(jnp.int32, (1, 128), 1)
    counts = jnp.zeros((1, 128), jnp.float32)
    for item in range(total):
        amount = target_ref[0, item].astype(jnp.float32)
        counts = counts + jnp.where(lane == task_ref[0, item], amount, 0.0)
    count_ref[...] = counts
    for tensor in range(2):
        into[tensor].wait()
        out[tensor].start()
    for tensor in range(2):
        out[tensor].wait()


def tabulate(me, lengths, targets, enc_pack, dec_pack, task, keys, values):
    rows, features = keys.shape
    half = features // 2
    return pl.pallas_call(
        table_kernel,
        out_shape=[
            jax.ShapeDtypeStruct((2, rows, half), keys.dtype),
            jax.ShapeDtypeStruct((4, FIELDS), jnp.int32),
            jax.ShapeDtypeStruct((1, 128), jnp.float32),
        ],
        in_specs=[SMEM] * 6 + [HBM] * 2,
        out_specs=[ANY, SMEM, VMEM],
        scratch_shapes=[pltpu.VMEM((2, rows, half), keys.dtype), pltpu.SemaphoreType.DMA((4,))],
        compiler_params=ROOM,
        cost_estimate=SMALL,
        name="tabulate",
    )(me, lengths, targets, enc_pack, dec_pack, task, keys, values)


def split_kernel(me_ref, q_ref, c_ref, own_ref, other_ref, held, sem):
    half = held.shape[-1]
    core = lax.rem(me_ref[0], 2)
    into, out = [], []
    for side, (base, target) in enumerate(((core, own_ref), (1 - core, other_ref))):
        columns = pl.ds(pl.multiple_of(base * half, PAIR), half)
        for tensor, source in enumerate((q_ref, c_ref)):
            place = 2 * side + tensor
            into.append(
                pltpu.make_async_copy(source.at[:, columns], held.at[place], sem.at[place])
            )
            out.append(
                pltpu.make_async_copy(held.at[place], target.at[tensor], sem.at[4 + place])
            )
    for copy in into:
        copy.start()
    for place in range(4):
        into[place].wait()
        out[place].start()
    for copy in out:
        copy.wait()


def split(me, queries, cotangent):
    rows, features = queries.shape
    half = features // 2
    return pl.pallas_call(
        split_kernel,
        out_shape=[jax.ShapeDtypeStruct((2, rows, half), queries.dtype)] * 2,
        in_specs=[SMEM] + [HBM] * 2,
        out_specs=[ANY] * 2,
        scratch_shapes=[
            pltpu.VMEM((4, rows, half), queries.dtype),
            pltpu.SemaphoreType.DMA((8,)),
        ],
        compiler_params=ROOM,
        cost_estimate=SMALL,
        name="split_columns",
    )(me, queries, cotangent)


def layout(packs):
    if packs == 8:
        return [(0, 2), (2, 2), (4, 2), (6, 1), (7, 1)]
    return [(first, 2) for first in range(0, packs, 2)]


def attention_kernel(
    me_ref, table_ref, scale_ref, *refs, packs, first, bases, half, at
):
    places = layout(packs)
    sources = len(places)
    pieces = refs[:packs]
    k_ref, v_ref, sibling_ref = refs[packs : packs + 3]
    outs = refs[packs + 3 + (0 if first else 3) :]
    k_out, v_out, sibling_out = outs[:3]
    query_outs = outs[3 : 3 + sources]
    loss_out = outs[3 + sources]
    kv, qc, dq, dkv, loss, scaling, in_sem, qc_sem, out_sem, dkv_sem = outs[sources + 4 :]
    width = qc.shape[-1]
    rows = qc.shape[2]
    keys = kv.shape[2]
    core = lax.rem(me_ref[0], 2)
    own_columns = pl.ds(pl.multiple_of(core * half + at, PAIR), width)
    half_columns = pl.ds(at, width)
    kv_copies = [
        [
            pltpu.make_async_copy(k_ref.at[:, own_columns], kv.at[0, 0], in_sem.at[0, 0]),
            pltpu.make_async_copy(v_ref.at[:, own_columns], kv.at[0, 1], in_sem.at[0, 1]),
        ],
        [
            pltpu.make_async_copy(
                sibling_ref.at[tensor, :, half_columns], kv.at[1, tensor], in_sem.at[1, tensor]
            )
            for tensor in range(2)
        ],
    ]
    dkv_copies = [
        [
            pltpu.make_async_copy(dkv.at[0, 0], k_out.at[:, own_columns], dkv_sem.at[0, 0]),
            pltpu.make_async_copy(dkv.at[0, 1], v_out.at[:, own_columns], dkv_sem.at[0, 1]),
        ],
        [
            pltpu.make_async_copy(
                dkv.at[1, tensor], sibling_out.at[tensor, :, half_columns], dkv_sem.at[1, tensor]
            )
            for tensor in range(2)
        ],
    ]
    for side in range(2):
        for copy in kv_copies[side]:
            copy.start()
        for place in range(2):
            item = 2 * side + place
            owner = table_ref[item, 0]
            for distance, piece in enumerate(pieces):

                @pl.when(owner == distance)
                def _(piece=piece, item=item, distance=distance):
                    pltpu.make_async_copy(
                        piece.at[:, :, pl.ds(at - bases[distance], width)],
                        qc.at[item],
                        qc_sem.at[item],
                    ).start()

    dq[...] = jnp.zeros_like(dq)
    loss[...] = jnp.zeros_like(loss)
    lane = lax.broadcasted_iota(jnp.int32, (1, PAIR), 1)
    low = lane < HEAD_DIM
    row = lax.broadcasted_iota(jnp.int32, (rows, PAIR), 0)
    row_lane = lax.broadcasted_iota(jnp.int32, (1, rows), 1)
    key = lax.broadcasted_iota(jnp.int32, (keys, 1), 0)
    key_lane = lax.broadcasted_iota(jnp.int32, (1, keys), 1)

    def dot(left, right):
        return jnp.dot(left, right, preferred_element_type=jnp.float32)

    vector = jnp.zeros((1, 128), jnp.float32)
    for side in range(2):
        for copy in kv_copies[side]:
            copy.wait()
        for place in range(2):
            item = 2 * side + place
            pltpu.make_async_copy(
                pieces[0].at[:, :, half_columns], qc.at[item], qc_sem.at[item]
            ).wait()
        owner, scale_rows = [], []
        border = table_ref[2 * side, 4]
        for place in range(2):
            item = 2 * side + place
            start, length = table_ref[item, 1], table_ref[item, 2]
            scale = scale_ref[0, table_ref[item, 5]]
            scaling[place] = jnp.where((row >= start) & (row < start + length), scale, 0.0)
            scale_rows.append(
                jnp.where((row_lane >= start) & (row_lane < start + length), scale, 0.0)
            )
            owner.append(table_ref[item, 0])

        def pair_chain(pair, side=side, owner=owner, scale_rows=scale_rows, border=border):
            columns = pl.ds(pl.multiple_of(pair * PAIR, PAIR), PAIR)
            early, early_lane = key < border, key_lane < border
            key_pair = kv[side, 0, :, columns]
            value_pair = kv[side, 1, :, columns]
            zero = jnp.zeros_like(key_pair)
            blank = jnp.zeros((HEAD_DIM, rows), key_pair.dtype)

            def by_example(array):
                return jnp.concatenate(
                    [jnp.where(early, array, zero), jnp.where(early, zero, array)], axis=1
                )

            def by_head(array):
                nothing = jnp.zeros_like(array)
                return jnp.concatenate(
                    [jnp.where(low, array, nothing), jnp.where(low, nothing, array)], axis=0
                )

            def spread(turned):
                blocks = []
                for array in turned:
                    blocks.append(jnp.concatenate([array[:HEAD_DIM], blank], axis=1))
                    blocks.append(jnp.concatenate([blank, array[HEAD_DIM:]], axis=1))
                return jnp.concatenate(blocks, axis=0)

            def example_parts(turned, part):
                array = turned[part]
                nothing = jnp.zeros_like(array)
                return jnp.concatenate(
                    [jnp.where(early_lane, array, nothing), jnp.where(early_lane, nothing, array)],
                    axis=0,
                )

            queries = [qc[2 * side + place, 0, :, columns] for place in range(2)]
            cots = [qc[2 * side + place, 1, :, columns] for place in range(2)]
            yield
            ups = [
                (cots[place].astype(jnp.float32) * scaling[place]).astype(jnp.bfloat16)
                for place in range(2)
            ]
            key_turned, value_turned = key_pair.T, value_pair.T
            cots_turned = [cot.T.astype(jnp.float32) for cot in cots]
            ups_turned = [
                (cots_turned[place] * scale_rows[place]).astype(jnp.bfloat16) for place in range(2)
            ]
            queries_turned = [query.T for query in queries]
            yield
            scores = dot(by_example(key_pair), spread(queries_turned))
            slopes = dot(by_example(value_pair), spread(ups_turned))
            yield
            lowest = jnp.float32(-3e38)
            highest = [
                jnp.max(jnp.where(early, scores, lowest), axis=0, keepdims=True),
                jnp.max(jnp.where(early, lowest, scores), axis=0, keepdims=True),
            ]
            yield
            powers = jnp.exp(scores - jnp.where(early, highest[0], highest[1]))
            inverse = [
                1.0 / jnp.sum(jnp.where(early, powers, 0.0), axis=0, keepdims=True),
                1.0 / jnp.sum(jnp.where(early, 0.0, powers), axis=0, keepdims=True),
            ]
            yield
            weights = powers * jnp.where(early, inverse[0], inverse[1])
            weights_low = weights.astype(jnp.bfloat16)
            yield
            drifts = [[], []]
            losses = []
            for head in range(2):
                part = slice(head * HEAD_DIM, (head + 1) * HEAD_DIM)
                lanes = slice(head * rows, (head + 1) * rows)
                attended = dot(example_parts(value_turned, part), weights_low[:, lanes])
                attended = attended.astype(jnp.bfloat16).astype(jnp.float32)
                for place in range(2):
                    item = 2 * side + place
                    here = attended[place * HEAD_DIM : (place + 1) * HEAD_DIM]
                    token = cots_turned[place][part] * here
                    losses.append(
                        (item, jnp.sum(token.reshape(HEAD_DIM // 8, 8, rows), axis=0))
                    )
                    drifts[place].append(
                        jnp.sum(
                            ups_turned[place][part].astype(jnp.float32) * here,
                            axis=0,
                            keepdims=True,
                        )
                    )
            yield
            drift = [jnp.concatenate(parts, axis=1) for parts in drifts]
            grad = weights * (slopes - jnp.where(early, drift[0], drift[1]))
            grad = grad.astype(jnp.bfloat16)
            yield
            query_parts = [[], []]
            for head in range(2):
                part = slice(head * HEAD_DIM, (head + 1) * HEAD_DIM)
                lanes = slice(head * rows, (head + 1) * rows)
                found = dot(example_parts(key_turned, part), grad[:, lanes])
                for place in range(2):
                    query_parts[place].append(found[place * HEAD_DIM : (place + 1) * HEAD_DIM])
            key_grad = dot(grad, jnp.concatenate([by_head(query) for query in queries], axis=1))
            value_grad = dot(weights_low, jnp.concatenate([by_head(up) for up in ups], axis=1))
            yield
            query_grads = [
                jnp.concatenate(query_parts[place], axis=0).astype(jnp.bfloat16).T
                for place in range(2)
            ]
            pair_grads = [
                jnp.where(early, found[:, :PAIR], found[:, PAIR:]).astype(jnp.bfloat16)
                for found in (key_grad, value_grad)
            ]
            yield
            for place in range(2):
                at = owner[place]
                dq[at, :, columns] = dq[at, :, columns] + query_grads[place]
            for tensor in range(2):
                dkv[side, tensor, :, columns] = pair_grads[tensor]
            for item, part in losses:
                loss[item] += part

        def group_step(group, carry, pair_chain=pair_chain):
            chains = [pair_chain(group * lockstep + i) for i in range(lockstep)]
            for _ in itertools.zip_longest(*chains):
                pass
            return carry

        lockstep = math.gcd(LOCKSTEP, width // PAIR)
        lax.fori_loop(0, width // PAIR // lockstep, group_step, 0)
        for copy in dkv_copies[side]:
            copy.start()
        for place in range(2):
            item = 2 * side + place
            start, length = table_ref[item, 1], table_ref[item, 2]
            part = jnp.sum(loss[item], axis=0, keepdims=True)
            part = jnp.where((row_lane >= start) & (row_lane < start + length), part, 0.0)
            amount = jnp.sum(part, axis=1, keepdims=True)
            vector = vector + jnp.where(lane == table_ref[item, 5], amount, 0.0)

    query_copies = [
        pltpu.make_async_copy(
            dq.at[pl.ds(base, 2)] if count == 2 else dq.at[base], target, out_sem.at[i]
        )
        for i, (target, (base, count)) in enumerate(zip(query_outs, places))
    ]
    for copy in query_copies:
        copy.start()
    loss_out[...] = vector
    for side in range(2):
        for copy in dkv_copies[side]:
            copy.wait()
    for copy in query_copies:
        copy.wait()


def attention_chunk(
    me, table, scales, pieces, keys, values, sibling, full, packs, bases, at, width
):
    sources = len(layout(packs))
    rows = pieces[0].shape[1]
    key_rows, features = keys.shape
    half = features // 2
    low = jnp.bfloat16
    first = full is None
    flops = rows * key_rows * width
    before = 3 + packs + 3
    return pl.pallas_call(
        functools.partial(
            attention_kernel,
            packs=packs,
            first=first,
            bases=bases,
            half=half,
            at=at,
        ),
        out_shape=[
            jax.ShapeDtypeStruct(keys.shape, low),
            jax.ShapeDtypeStruct(keys.shape, low),
            jax.ShapeDtypeStruct((2, key_rows, half), low),
        ]
        + [
            jax.ShapeDtypeStruct((count, rows, width)[2 - count :], low)
            for _, count in layout(packs)
        ]
        + [jax.ShapeDtypeStruct((1, 128), jnp.float32)],
        in_specs=[SMEM] * 3 + [ANY] * packs + [HBM] * 2 + [ANY] + [HBM] * (0 if first else 3),
        out_specs=[HBM] * 3 + [ANY] * sources + [VMEM],
        scratch_shapes=[
            pltpu.VMEM((2, 2, key_rows, width), low),
            pltpu.VMEM((4, 2, rows, width), low),
            pltpu.VMEM((packs, rows, width), low),
            pltpu.VMEM((2, 2, key_rows, width), low),
            pltpu.VMEM((4, 8, rows), jnp.float32),
            pltpu.VMEM((2, rows, PAIR), jnp.float32),
            pltpu.SemaphoreType.DMA((2, 2)),
            pltpu.SemaphoreType.DMA((4,)),
            pltpu.SemaphoreType.DMA((sources,)),
            pltpu.SemaphoreType.DMA((2, 2)),
        ],
        input_output_aliases={} if first else {before + i: i for i in range(3)},
        compiler_params=pltpu.CompilerParams(
            vmem_limit_bytes=14 * 1024 * 1024 + 2 * packs * rows * width
        ),
        cost_estimate=pl.CostEstimate(
            flops=flops, bytes_accessed=8 * 1024 * 1024, transcendentals=0
        ),
        name="attention_chunk",
    )(me, table, scales, *pieces, keys, values, sibling, *(() if first else full))


def finish_kernel(me_ref, *refs, spots, half, with_keys):
    count = 2 * len(spots)
    outs = refs[-1 - (3 if with_keys else 1) : -1]
    sem = refs[-1]
    core = lax.rem(me_ref[0], 2)
    moves = []
    for i, (at, width) in enumerate(spots):
        for side, base in enumerate((core, 1 - core)):
            columns = pl.ds(pl.multiple_of(base * half + at, PAIR), width)
            moves.append((refs[2 * i + side], outs[0], columns))
    if with_keys:
        other = pl.ds(pl.multiple_of((1 - core) * half, PAIR), half)
        moves += [(refs[count].at[tensor], outs[1 + tensor], other) for tensor in range(2)]
    copies = [
        pltpu.make_async_copy(source, out.at[:, columns], sem.at[i])
        for i, (source, out, columns) in enumerate(moves)
    ]
    for copy in copies:
        copy.start()
    for copy in copies:
        copy.wait()


def finish(me, parts, spots, like, back=None, given=()):
    with_keys = back is not None
    read = len(parts) + (1 if with_keys else 0)
    shapes = [jax.ShapeDtypeStruct(like.shape, like.dtype)]
    if with_keys:
        shapes += [jax.ShapeDtypeStruct(array.shape, array.dtype) for array in given]
    skipped = len(shapes) - len(given)
    return pl.pallas_call(
        functools.partial(
            finish_kernel, spots=spots, half=like.shape[1] // 2, with_keys=with_keys
        ),
        out_shape=shapes,
        in_specs=[SMEM] + [VMEM] * read + [HBM] * len(given),
        out_specs=[HBM] * len(shapes),
        scratch_shapes=[pltpu.SemaphoreType.DMA((len(parts) + 2,))],
        input_output_aliases={1 + read + i: skipped + i for i in range(len(given))},
        compiler_params=ROOM,
        cost_estimate=SMALL,
        name="finish",
    )(me, *parts, *((back,) if with_keys else ()), *given)


def swap(array, axis_name, size, bits):
    return lax.ppermute(array, axis_name, [(i, i ^ bits) for i in range(size)])


def doubled_sum(array, axis_name, size, first=1, last=None):
    step = first
    while step < (last or size):
        array = array + swap(array, axis_name, size, step)
        step *= 2
    return array


together = lax.optimization_barrier


def local(
    enc_keys,
    enc_values,
    dec_queries,
    cotangent,
    input_lengths,
    target_lengths,
    enc_pack,
    dec_pack,
    task_group,
    dro_weights,
    *,
    packs,
    groups,
):
    me = lax.axis_index("pack").astype(jnp.int32).reshape(1)
    rows, features = dec_queries.shape
    half = features // 2
    total_tokens = rows * packs * groups
    relayed = packs == 8

    def swapped(array, bits):
        return swap(array, "pack", packs, bits)

    def tabulated(me):
        return tabulate(
            me,
            input_lengths,
            target_lengths,
            enc_pack,
            dec_pack,
            task_group[:, :, 0],
            enc_keys,
            enc_values,
        )

    def scales_of(group_counts):
        counts = doubled_sum(group_counts, "dp", groups)
        weights = dro_weights.astype(jnp.float32)
        weights = jnp.pad(weights, (0, 128 - GROUPS)).reshape(1, 128)
        return counts, weights / jnp.sum(weights) * (total_tokens / counts)

    widths = [half * share // sum(CHUNKS) for share in CHUNKS]
    starts = [sum(widths[:i]) for i in range(len(widths))]
    spots = list(zip(starts, widths))
    own, other = split(me, dec_queries, cotangent)
    if not relayed:
        pieces = [own] + [swapped(other if i & 1 else own, i) for i in range(1, packs)]
        kv_other, table, group_counts = tabulated(me)
        kv_sibling = swapped(kv_other, 1)
        counts, scales = scales_of(group_counts)
        full, losses, query_parts = None, [], []
        for at, width in spots:
            *result, loss = attention_chunk(
                me, table, scales, pieces, enc_keys, enc_values, kv_sibling, full,
                packs, [0] * packs, at, width,
            )
            full, parts = result[:3], result[3:]
            losses.append(loss)
            summed = parts[0]
            for chip in range(1, len(parts)):
                summed = summed + swapped(parts[chip], 2 * chip)
            query_parts += [summed[0], swapped(summed[1], 1)]
        back = swapped(full[2], 1)
        loss = doubled_sum(functools.reduce(jnp.add, losses), "pack", packs)
        loss = doubled_sum(loss, "dp", groups)
    else:
        first = widths[0]
        x_own, y_own = swapped(own, 2), swapped(own, 4)
        x_other, y_other = swapped(other, 3), swapped(other, 5)
        sibling = swapped(other, 1)
        me_later, x_own = together((me, x_own))
        kv_other, table, group_counts = tabulated(me_later)
        near = [x_own[:, :, :first], x_own[:, :, first:]]
        x_own, y_own, x_other, y_other, sibling, kv_other, group_counts, table, near = together(
            (x_own, y_own, x_other, y_other, sibling, kv_other, group_counts, table, near)
        )
        far = [y_other[:, :, :first], y_other[:, :, first:]]
        diagonal = [swapped(near[0], 4), swapped(far[0], 2)]
        kv_sibling = swapped(kv_other, 1)
        counts, scales = scales_of(group_counts)
        diagonal, near, far, kv_sibling, scales = together(
            (diagonal, near, far, kv_sibling, scales)
        )
        later = [swapped(near[1], 4), swapped(far[1], 2)]

        def attend(full, chunk, diagonal, base):
            at, width = spots[chunk]
            pieces = [own, sibling, x_own, x_other, y_own, y_other, *diagonal]
            *result, loss = attention_chunk(
                me, table, scales, pieces, enc_keys, enc_values, kv_sibling, full,
                packs, [0] * 6 + [base] * 2, at, width,
            )
            return result[:3], result[3:], loss

        def forwarded(parts):
            return [swapped(parts[3], 2), swapped(parts[4], 4)]

        def merged(parts, relay):
            via_x, via_y = relay
            to_y = parts[2] + jnp.stack([via_x, jnp.zeros_like(via_x)])
            to_x = parts[1] + jnp.stack([jnp.zeros_like(via_y), via_y])
            return [swapped(to_x, 2), swapped(to_y, 4)]

        def total(parts, arrived):
            return parts[0] + arrived[0] + arrived[1]

        full, parts_a, loss_a = attend(None, 0, diagonal, 0)
        later, full, parts_a = together((later, full, parts_a))

        relay_a = forwarded(parts_a)
        full, parts_b, loss_b = attend(full, 1, later, first)
        relay_a, full, parts_b = together((relay_a, full, parts_b))

        arrived_a = merged(parts_a, relay_a)
        relay_b = forwarded(parts_b)
        loss = doubled_sum(doubled_sum(loss_a + loss_b, "dp", groups), "pack", packs, 1, 2)
        arrived_a, relay_b, loss = together((arrived_a, relay_b, loss))

        arrived_b = merged(parts_b, relay_b)
        total_a = total(parts_a, arrived_a)
        query_parts = [total_a[0], swapped(total_a[1], 1)]
        back = swapped(full[2], 1)
        arrived_b, query_parts, back = together((arrived_b, query_parts, back))

        total_b = total(parts_b, arrived_b)
        query_parts += [total_b[0], swapped(total_b[1], 1)]
        loss = doubled_sum(loss, "pack", packs, 2)

    queries_gradient, keys_gradient, values_gradient = finish(
        me, query_parts[:-2], spots[:-1], dec_queries, back, full[:2]
    )
    (queries_gradient,) = finish(
        me, query_parts[-2:], spots[-1:], dec_queries, None, (queries_gradient,)
    )
    group_loss = (loss / counts)[0, :GROUPS]
    return (queries_gradient, keys_gradient, values_gradient, group_loss)


def solution(mesh):
    placed = (
        P(("dp", "pack"), None),
        P(("dp", "pack"), None),
        P(("dp", "pack"), None),
        P(("dp", "pack"), None),
        P("dp", None),
        P("dp", None),
        P("dp", None),
        P("dp", None),
        P("dp", None, None),
        P(),
    )
    return jax.shard_map(
        functools.partial(local, packs=mesh.shape["pack"], groups=mesh.shape["dp"]),
        mesh=mesh,
        in_specs=placed,
        out_specs=(P(("dp", "pack"), None), P(("dp", "pack"), None), P(("dp", "pack"), None), P()),
        check_vma=False,
    )
```

```python
import functools
import itertools
import math

import jax
import jax.numpy as jnp
from jax import lax
from jax.experimental import pallas as pl
from jax.experimental.pallas import tpu as pltpu
from jax.sharding import PartitionSpec as P

HEAD_DIM = 64
PAIR = 2 * HEAD_DIM
EX_DEV = 2
GROUPS = 16
CHUNKS = (1, 1)
LOCKSTEP = 4
ALONE = pltpu.CompilerParams(vmem_limit_bytes=60 * 1024 * 1024)
ROOM = pltpu.CompilerParams(vmem_limit_bytes=16 * 1024 * 1024)
FIELDS = 8
SMALL = pl.CostEstimate(flops=0, bytes_accessed=2 * 1024 * 1024, transcendentals=0)
ANY = pl.BlockSpec(memory_space=pl.ANY)
HBM = pl.BlockSpec(memory_space=pltpu.HBM)
SMEM = pl.BlockSpec(memory_space=pltpu.SMEM)
VMEM = pl.BlockSpec(memory_space=pltpu.VMEM)


def table_kernel(
    me_ref,
    input_ref,
    target_ref,
    enc_ref,
    dec_ref,
    task_ref,
    k_ref,
    v_ref,
    *refs,
):
    kv_ref, table_ref, count_ref, held, sem = refs[-5:]
    me = me_ref[0]
    core = lax.rem(me, 2)
    half = held.shape[-1]
    columns = pl.ds(pl.multiple_of((1 - core) * half, half), half)
    into = [
        pltpu.make_async_copy(source.at[:, columns], held.at[tensor], sem.at[tensor])
        for tensor, source in enumerate((k_ref, v_ref))
    ]
    out = [
        pltpu.make_async_copy(held.at[tensor], kv_ref.at[tensor], sem.at[2 + tensor])
        for tensor in range(2)
    ]
    for copy in into:
        copy.start()
    total = enc_ref.shape[1]
    for side in range(2):
        pack = me + side * (1 - 2 * core)

        def find(item, carry, pack=pack):
            first, second = carry
            hit = enc_ref[0, item] == pack
            return (
                jnp.where(hit & (first < 0), item, first),
                jnp.where(hit & (first >= 0), item, second),
            )

        first, second = lax.fori_loop(0, total, find, (jnp.int32(-1), jnp.int32(-1)))
        second = jnp.maximum(second, 0)
        first = jnp.maximum(first, 0)
        for place, item in enumerate((first, second)):
            row = 2 * side + place
            dec = dec_ref[0, item]

            def before(other, offset, dec=dec):
                return offset + jnp.where(dec_ref[0, other] == dec, target_ref[0, other], 0)

            table_ref[row, 0] = dec ^ me
            table_ref[row, 1] = lax.fori_loop(0, item, before, jnp.int32(0))
            table_ref[row, 2] = target_ref[0, item]
            table_ref[row, 3] = jnp.int32(0) if place == 0 else input_ref[0, first]
            table_ref[row, 4] = input_ref[0, item]
            table_ref[row, 5] = task_ref[0, item]
            table_ref[row, 6] = 0
            table_ref[row, 7] = 0
    lane = lax.broadcasted_iota(jnp.int32, (1, 128), 1)
    counts = jnp.zeros((1, 128), jnp.float32)
    for item in range(total):
        amount = target_ref[0, item].astype(jnp.float32)
        counts = counts + jnp.where(lane == task_ref[0, item], amount, 0.0)
    count_ref[...] = counts
    for tensor in range(2):
        into[tensor].wait()
        out[tensor].start()
    for tensor in range(2):
        out[tensor].wait()


def tabulate(me, lengths, targets, enc_pack, dec_pack, task, keys, values):
    rows, features = keys.shape
    half = features // 2
    return pl.pallas_call(
        table_kernel,
        out_shape=[
            jax.ShapeDtypeStruct((2, rows, half), keys.dtype),
            jax.ShapeDtypeStruct((4, FIELDS), jnp.int32),
            jax.ShapeDtypeStruct((1, 128), jnp.float32),
        ],
        in_specs=[SMEM] * 6 + [HBM] * 2,
        out_specs=[ANY, SMEM, VMEM],
        scratch_shapes=[pltpu.VMEM((2, rows, half), keys.dtype), pltpu.SemaphoreType.DMA((4,))],
        compiler_params=ROOM,
        cost_estimate=SMALL,
        name="tabulate",
    )(me, lengths, targets, enc_pack, dec_pack, task, keys, values)


def split_kernel(me_ref, q_ref, c_ref, own_ref, other_ref, held, sem):
    half = held.shape[-1]
    core = lax.rem(me_ref[0], 2)
    into, out = [], []
    for side, (base, target) in enumerate(((core, own_ref), (1 - core, other_ref))):
        columns = pl.ds(pl.multiple_of(base * half, PAIR), half)
        for tensor, source in enumerate((q_ref, c_ref)):
            place = 2 * side + tensor
            into.append(
                pltpu.make_async_copy(source.at[:, columns], held.at[place], sem.at[place])
            )
            out.append(
                pltpu.make_async_copy(held.at[place], target.at[tensor], sem.at[4 + place])
            )
    for copy in into:
        copy.start()
    for place in range(4):
        into[place].wait()
        out[place].start()
    for copy in out:
        copy.wait()


def split(me, queries, cotangent):
    rows, features = queries.shape
    half = features // 2
    return pl.pallas_call(
        split_kernel,
        out_shape=[jax.ShapeDtypeStruct((2, rows, half), queries.dtype)] * 2,
        in_specs=[SMEM] + [HBM] * 2,
        out_specs=[ANY] * 2,
        scratch_shapes=[
            pltpu.VMEM((4, rows, half), queries.dtype),
            pltpu.SemaphoreType.DMA((8,)),
        ],
        compiler_params=ROOM,
        cost_estimate=SMALL,
        name="split_columns",
    )(me, queries, cotangent)


def attention_kernel(
    me_ref, table_ref, scale_ref, *refs, packs, first, bases, half, at
):
    pieces = refs[:packs]
    k_ref, v_ref, sibling_ref = refs[packs : packs + 3]
    outs = refs[packs + 3 + (0 if first else 3) :]
    k_out, v_out, sibling_out = outs[:3]
    query_outs = outs[3 : 3 + packs]
    loss_out = outs[3 + packs]
    kv, qc, dq, dkv, loss, scaling, in_sem, qc_sem, out_sem, dkv_sem = outs[packs + 4 :]
    width = qc.shape[-1]
    rows = qc.shape[2]
    keys = kv.shape[2]
    core = lax.rem(me_ref[0], 2)
    own_columns = pl.ds(pl.multiple_of(core * half + at, PAIR), width)
    half_columns = pl.ds(at, width)
    kv_copies = [
        [
            pltpu.make_async_copy(k_ref.at[:, own_columns], kv.at[0, 0], in_sem.at[0, 0]),
            pltpu.make_async_copy(v_ref.at[:, own_columns], kv.at[0, 1], in_sem.at[0, 1]),
        ],
        [
            pltpu.make_async_copy(
                sibling_ref.at[tensor, :, half_columns], kv.at[1, tensor], in_sem.at[1, tensor]
            )
            for tensor in range(2)
        ],
    ]
    dkv_copies = [
        [
            pltpu.make_async_copy(dkv.at[0, 0], k_out.at[:, own_columns], dkv_sem.at[0, 0]),
            pltpu.make_async_copy(dkv.at[0, 1], v_out.at[:, own_columns], dkv_sem.at[0, 1]),
        ],
        [
            pltpu.make_async_copy(
                dkv.at[1, tensor], sibling_out.at[tensor, :, half_columns], dkv_sem.at[1, tensor]
            )
            for tensor in range(2)
        ],
    ]
    for side in range(2):
        for copy in kv_copies[side]:
            copy.start()
        for place in range(2):
            item = 2 * side + place
            owner = table_ref[item, 0]
            for distance, piece in enumerate(pieces):

                @pl.when(owner == distance)
                def _(piece=piece, item=item, distance=distance):
                    pltpu.make_async_copy(
                        piece.at[:, :, pl.ds(at - bases[distance], width)],
                        qc.at[item],
                        qc_sem.at[item],
                    ).start()

    dq[...] = jnp.zeros_like(dq)
    loss[...] = jnp.zeros_like(loss)
    lane = lax.broadcasted_iota(jnp.int32, (1, PAIR), 1)
    low = lane < HEAD_DIM
    row = lax.broadcasted_iota(jnp.int32, (rows, PAIR), 0)
    row_lane = lax.broadcasted_iota(jnp.int32, (1, rows), 1)
    key = lax.broadcasted_iota(jnp.int32, (keys, 1), 0)
    key_lane = lax.broadcasted_iota(jnp.int32, (1, keys), 1)

    def dot(left, right):
        return jnp.dot(left, right, preferred_element_type=jnp.float32)

    vector = jnp.zeros((1, 128), jnp.float32)
    for side in range(2):
        for copy in kv_copies[side]:
            copy.wait()
        for place in range(2):
            item = 2 * side + place
            pltpu.make_async_copy(
                pieces[0].at[:, :, half_columns], qc.at[item], qc_sem.at[item]
            ).wait()
        owner, scale_rows = [], []
        border = table_ref[2 * side, 4]
        for place in range(2):
            item = 2 * side + place
            start, length = table_ref[item, 1], table_ref[item, 2]
            scale = scale_ref[0, table_ref[item, 5]]
            scaling[place] = jnp.where((row >= start) & (row < start + length), scale, 0.0)
            scale_rows.append(
                jnp.where((row_lane >= start) & (row_lane < start + length), scale, 0.0)
            )
            owner.append(table_ref[item, 0])

        def pair_chain(pair, side=side, owner=owner, scale_rows=scale_rows, border=border):
            columns = pl.ds(pl.multiple_of(pair * PAIR, PAIR), PAIR)
            early, early_lane = key < border, key_lane < border
            key_pair = kv[side, 0, :, columns]
            value_pair = kv[side, 1, :, columns]
            zero = jnp.zeros_like(key_pair)
            blank = jnp.zeros((HEAD_DIM, rows), key_pair.dtype)

            def by_example(array):
                return jnp.concatenate(
                    [jnp.where(early, array, zero), jnp.where(early, zero, array)], axis=1
                )

            def by_head(array):
                nothing = jnp.zeros_like(array)
                return jnp.concatenate(
                    [jnp.where(low, array, nothing), jnp.where(low, nothing, array)], axis=0
                )

            def spread(turned):
                blocks = []
                for array in turned:
                    blocks.append(jnp.concatenate([array[:HEAD_DIM], blank], axis=1))
                    blocks.append(jnp.concatenate([blank, array[HEAD_DIM:]], axis=1))
                return jnp.concatenate(blocks, axis=0)

            def example_parts(turned, part):
                array = turned[part]
                nothing = jnp.zeros_like(array)
                return jnp.concatenate(
                    [jnp.where(early_lane, array, nothing), jnp.where(early_lane, nothing, array)],
                    axis=0,
                )

            queries = [qc[2 * side + place, 0, :, columns] for place in range(2)]
            cots = [qc[2 * side + place, 1, :, columns] for place in range(2)]
            yield
            ups = [
                (cots[place].astype(jnp.float32) * scaling[place]).astype(jnp.bfloat16)
                for place in range(2)
            ]
            key_turned, value_turned = key_pair.T, value_pair.T
            cots_turned = [cot.T.astype(jnp.float32) for cot in cots]
            ups_turned = [
                (cots_turned[place] * scale_rows[place]).astype(jnp.bfloat16) for place in range(2)
            ]
            queries_turned = [query.T for query in queries]
            yield
            scores = dot(by_example(key_pair), spread(queries_turned))
            slopes = dot(by_example(value_pair), spread(ups_turned))
            yield
            lowest = jnp.float32(-3e38)
            highest = [
                jnp.max(jnp.where(early, scores, lowest), axis=0, keepdims=True),
                jnp.max(jnp.where(early, lowest, scores), axis=0, keepdims=True),
            ]
            yield
            powers = jnp.exp(scores - jnp.where(early, highest[0], highest[1]))
            inverse = [
                1.0 / jnp.sum(jnp.where(early, powers, 0.0), axis=0, keepdims=True),
                1.0 / jnp.sum(jnp.where(early, 0.0, powers), axis=0, keepdims=True),
            ]
            yield
            weights = powers * jnp.where(early, inverse[0], inverse[1])
            weights_low = weights.astype(jnp.bfloat16)
            yield
            drifts = [[], []]
            losses = []
            for head in range(2):
                part = slice(head * HEAD_DIM, (head + 1) * HEAD_DIM)
                lanes = slice(head * rows, (head + 1) * rows)
                attended = dot(example_parts(value_turned, part), weights_low[:, lanes])
                attended = attended.astype(jnp.bfloat16).astype(jnp.float32)
                for place in range(2):
                    item = 2 * side + place
                    here = attended[place * HEAD_DIM : (place + 1) * HEAD_DIM]
                    token = cots_turned[place][part] * here
                    losses.append(
                        (item, jnp.sum(token.reshape(HEAD_DIM // 8, 8, rows), axis=0))
                    )
                    drifts[place].append(
                        jnp.sum(
                            ups_turned[place][part].astype(jnp.float32) * here,
                            axis=0,
                            keepdims=True,
                        )
                    )
            yield
            drift = [jnp.concatenate(parts, axis=1) for parts in drifts]
            grad = weights * (slopes - jnp.where(early, drift[0], drift[1]))
            grad = grad.astype(jnp.bfloat16)
            yield
            query_parts = [[], []]
            for head in range(2):
                part = slice(head * HEAD_DIM, (head + 1) * HEAD_DIM)
                lanes = slice(head * rows, (head + 1) * rows)
                found = dot(example_parts(key_turned, part), grad[:, lanes])
                for place in range(2):
                    query_parts[place].append(found[place * HEAD_DIM : (place + 1) * HEAD_DIM])
            key_grad = dot(grad, jnp.concatenate([by_head(query) for query in queries], axis=1))
            value_grad = dot(weights_low, jnp.concatenate([by_head(up) for up in ups], axis=1))
            yield
            query_grads = [
                jnp.concatenate(query_parts[place], axis=0).astype(jnp.bfloat16).T
                for place in range(2)
            ]
            pair_grads = [
                jnp.where(early, found[:, :PAIR], found[:, PAIR:]).astype(jnp.bfloat16)
                for found in (key_grad, value_grad)
            ]
            yield
            for place in range(2):
                at = owner[place]
                dq[at, :, columns] = dq[at, :, columns] + query_grads[place]
            for tensor in range(2):
                dkv[side, tensor, :, columns] = pair_grads[tensor]
            for item, part in losses:
                loss[item] += part

        def group_step(group, carry, pair_chain=pair_chain):
            chains = [pair_chain(group * lockstep + i) for i in range(lockstep)]
            for _ in itertools.zip_longest(*chains):
                pass
            return carry

        lockstep = math.gcd(LOCKSTEP, width // PAIR)
        lax.fori_loop(0, width // PAIR // lockstep, group_step, 0)
        for copy in dkv_copies[side]:
            copy.start()
        for place in range(2):
            item = 2 * side + place
            start, length = table_ref[item, 1], table_ref[item, 2]
            part = jnp.sum(loss[item], axis=0, keepdims=True)
            part = jnp.where((row_lane >= start) & (row_lane < start + length), part, 0.0)
            amount = jnp.sum(part, axis=1, keepdims=True)
            vector = vector + jnp.where(lane == table_ref[item, 5], amount, 0.0)

    query_copies = [
        pltpu.make_async_copy(dq.at[distance], target, out_sem.at[distance])
        for distance, target in enumerate(query_outs)
    ]
    for copy in query_copies:
        copy.start()
    loss_out[...] = vector
    for side in range(2):
        for copy in dkv_copies[side]:
            copy.wait()
    for copy in query_copies:
        copy.wait()


def attention_chunk(
    me, table, scales, pieces, keys, values, sibling, full, packs, bases, at, width
):
    rows = pieces[0].shape[1]
    key_rows, features = keys.shape
    half = features // 2
    low = jnp.bfloat16
    first = full is None
    flops = rows * key_rows * width
    before = 3 + packs + 3
    return pl.pallas_call(
        functools.partial(
            attention_kernel,
            packs=packs,
            first=first,
            bases=bases,
            half=half,
            at=at,
        ),
        out_shape=[
            jax.ShapeDtypeStruct(keys.shape, low),
            jax.ShapeDtypeStruct(keys.shape, low),
            jax.ShapeDtypeStruct((2, key_rows, half), low),
        ]
        + [jax.ShapeDtypeStruct((rows, width), low)] * packs
        + [jax.ShapeDtypeStruct((1, 128), jnp.float32)],
        in_specs=[SMEM] * 3 + [ANY] * packs + [HBM] * 2 + [ANY] + [HBM] * (0 if first else 3),
        out_specs=[HBM] * 3 + [ANY] * packs + [VMEM],
        scratch_shapes=[
            pltpu.VMEM((2, 2, key_rows, width), low),
            pltpu.VMEM((4, 2, rows, width), low),
            pltpu.VMEM((packs, rows, width), low),
            pltpu.VMEM((2, 2, key_rows, width), low),
            pltpu.VMEM((4, 8, rows), jnp.float32),
            pltpu.VMEM((2, rows, PAIR), jnp.float32),
            pltpu.SemaphoreType.DMA((2, 2)),
            pltpu.SemaphoreType.DMA((4,)),
            pltpu.SemaphoreType.DMA((packs,)),
            pltpu.SemaphoreType.DMA((2, 2)),
        ],
        input_output_aliases={} if first else {before + i: i for i in range(3)},
        compiler_params=pltpu.CompilerParams(
            vmem_limit_bytes=14 * 1024 * 1024 + 2 * packs * rows * width
        ),
        cost_estimate=pl.CostEstimate(
            flops=flops, bytes_accessed=8 * 1024 * 1024, transcendentals=0
        ),
        name="attention_chunk",
    )(me, table, scales, *pieces, keys, values, sibling, *(() if first else full))


def finish_kernel(me_ref, *refs, terms, at, half, with_keys):
    near, far = refs[:terms], refs[terms : 2 * terms]
    outs = refs[-2 - (3 if with_keys else 1) : -2]
    merged, sem = refs[-2:]
    width = merged.shape[-1]
    core = lax.rem(me_ref[0], 2)
    copies = []
    if with_keys:
        other = pl.ds(pl.multiple_of((1 - core) * half, PAIR), half)
        for tensor in range(2):
            copies.append(
                pltpu.make_async_copy(
                    refs[2 * terms].at[tensor], outs[1 + tensor].at[:, other], sem.at[tensor]
                )
            )
            copies[-1].start()
    for side, (base, parts) in enumerate(((core, near), (1 - core, far))):
        columns = pl.ds(pl.multiple_of(base * half + at, PAIR), width)
        merged[side] = functools.reduce(jnp.add, [part[...] for part in parts])
        copies.append(
            pltpu.make_async_copy(merged.at[side], outs[0].at[:, columns], sem.at[2 + side])
        )
        copies[-1].start()
    for copy in copies:
        copy.wait()


def finish(me, near, far, at, like, back=None, given=()):
    with_keys = back is not None
    read = 2 * len(near) + (1 if with_keys else 0)
    shapes = [jax.ShapeDtypeStruct(like.shape, like.dtype)]
    if with_keys:
        shapes += [jax.ShapeDtypeStruct(array.shape, array.dtype) for array in given]
    skipped = len(shapes) - len(given)
    return pl.pallas_call(
        functools.partial(
            finish_kernel, terms=len(near), at=at, half=like.shape[1] // 2, with_keys=with_keys
        ),
        out_shape=shapes,
        in_specs=[SMEM] + [VMEM] * read + [HBM] * len(given),
        out_specs=[HBM] * len(shapes),
        scratch_shapes=[
            pltpu.VMEM((2, *near[0].shape), like.dtype),
            pltpu.SemaphoreType.DMA((4,)),
        ],
        input_output_aliases={1 + read + i: skipped + i for i in range(len(given))},
        compiler_params=ROOM,
        cost_estimate=SMALL,
        name="finish",
    )(me, *near, *far, *((back,) if with_keys else ()), *given)


def swap(array, axis_name, size, bits):
    return lax.ppermute(array, axis_name, [(i, i ^ bits) for i in range(size)])


def doubled_sum(array, axis_name, size, first=1, last=None):
    step = first
    while step < (last or size):
        array = array + swap(array, axis_name, size, step)
        step *= 2
    return array


together = lax.optimization_barrier


def local(
    enc_keys,
    enc_values,
    dec_queries,
    cotangent,
    input_lengths,
    target_lengths,
    enc_pack,
    dec_pack,
    task_group,
    dro_weights,
    *,
    packs,
    groups,
):
    me = lax.axis_index("pack").astype(jnp.int32).reshape(1)
    rows, features = dec_queries.shape
    half = features // 2
    total_tokens = rows * packs * groups
    relayed = packs == 8

    def swapped(array, bits):
        return swap(array, "pack", packs, bits)

    def tabulated(me):
        return tabulate(
            me,
            input_lengths,
            target_lengths,
            enc_pack,
            dec_pack,
            task_group[:, :, 0],
            enc_keys,
            enc_values,
        )

    def scales_of(group_counts):
        counts = doubled_sum(group_counts, "dp", groups)
        weights = dro_weights.astype(jnp.float32)
        weights = jnp.pad(weights, (0, 128 - GROUPS)).reshape(1, 128)
        return counts, weights / jnp.sum(weights) * (total_tokens / counts)

    widths = [half * share // sum(CHUNKS) for share in CHUNKS]
    starts = [sum(widths[:i]) for i in range(len(widths))]
    spots = list(zip(starts, widths))
    own, other = split(me, dec_queries, cotangent)
    if not relayed:
        pieces = [own] + [swapped(other if i & 1 else own, i) for i in range(1, packs)]
        kv_other, table, group_counts = tabulated(me)
        kv_sibling = swapped(kv_other, 1)
        counts, scales = scales_of(group_counts)
        full, losses, ends = None, [], []
        for at, width in spots:
            *result, loss = attention_chunk(
                me, table, scales, pieces, enc_keys, enc_values, kv_sibling, full,
                packs, [0] * packs, at, width,
            )
            full, parts = result[:3], result[3:]
            losses.append(loss)
            arrived = parts[:1] + [swapped(parts[i], i) for i in range(1, packs)]
            ends.append((arrived[0::2], arrived[1::2]))
        back = swapped(full[2], 1)
        loss = doubled_sum(functools.reduce(jnp.add, losses), "pack", packs)
        loss = doubled_sum(loss, "dp", groups)
    else:
        first = widths[0]
        x_own, y_own = swapped(own, 2), swapped(own, 4)
        x_other, y_other = swapped(other, 3), swapped(other, 5)
        sibling = swapped(other, 1)
        me_later, x_own = together((me, x_own))
        kv_other, table, group_counts = tabulated(me_later)
        near = [x_own[:, :, :first], x_own[:, :, first:]]
        x_own, y_own, x_other, y_other, sibling, kv_other, group_counts, table, near = together(
            (x_own, y_own, x_other, y_other, sibling, kv_other, group_counts, table, near)
        )
        far = [y_other[:, :, :first], y_other[:, :, first:]]
        diagonal = [swapped(near[0], 4), swapped(far[0], 2)]
        kv_sibling = swapped(kv_other, 1)
        counts, scales = scales_of(group_counts)
        diagonal, near, far, kv_sibling, scales = together(
            (diagonal, near, far, kv_sibling, scales)
        )
        later = [swapped(near[1], 4), swapped(far[1], 2)]

        def attend(full, chunk, diagonal, base):
            at, width = spots[chunk]
            pieces = [own, sibling, x_own, x_other, y_own, y_other, *diagonal]
            *result, loss = attention_chunk(
                me, table, scales, pieces, enc_keys, enc_values, kv_sibling, full,
                packs, [0] * 6 + [base] * 2, at, width,
            )
            return result[:3], result[3:], loss

        def forwarded(parts):
            return [swapped(parts[6], 2), swapped(parts[7], 4)]

        def sent(parts):
            return [swapped(parts[2], 2), swapped(parts[5], 5), swapped(parts[1], 1)]

        def merged(parts, relay):
            return [swapped(parts[4] + relay[0], 4), swapped(parts[3] + relay[1], 3)]

        def sums(parts, direct, last):
            return [parts[0], direct[0], last[0]], [direct[2], direct[1], last[1]]

        full, parts_a, loss_a = attend(None, 0, diagonal, 0)
        later, full, parts_a = together((later, full, parts_a))

        relay_a, direct_a = forwarded(parts_a), sent(parts_a)
        full, parts_b, loss_b = attend(full, 1, later, first)
        relay_a, direct_a, full, parts_b, loss_b = together(
            (relay_a, direct_a, full, parts_b, loss_b)
        )

        last_a, relay_b = merged(parts_a, relay_a), forwarded(parts_b)
        loss = doubled_sum(loss_a + loss_b, "dp", groups)
        loss = doubled_sum(loss, "pack", packs, 1, 4)
        last_a, relay_b, loss, full = together((last_a, relay_b, loss, full))

        last_b, direct_b = merged(parts_b, relay_b), sent(parts_b)
        back = swapped(full[2], 1)
        loss = doubled_sum(loss, "pack", packs, 4)
        last_b, direct_b, back, loss = together((last_b, direct_b, back, loss))
        ends = [sums(parts_a, direct_a, last_a), sums(parts_b, direct_b, last_b)]

    queries_gradient, keys_gradient, values_gradient = finish(
        me, *ends[0], starts[0], dec_queries, back, full[:2]
    )
    for (at, _), end in zip(spots[1:], ends[1:]):
        (queries_gradient,) = finish(me, *end, at, dec_queries, None, (queries_gradient,))
    group_loss = (loss / counts)[0, :GROUPS]
    return (queries_gradient, keys_gradient, values_gradient, group_loss)


def solution(mesh):
    placed = (
        P(("dp", "pack"), None),
        P(("dp", "pack"), None),
        P(("dp", "pack"), None),
        P(("dp", "pack"), None),
        P("dp", None),
        P("dp", None),
        P("dp", None),
        P("dp", None),
        P("dp", None, None),
        P(),
    )
    return jax.shard_map(
        functools.partial(local, packs=mesh.shape["pack"], groups=mesh.shape["dp"]),
        mesh=mesh,
        in_specs=placed,
        out_specs=(P(("dp", "pack"), None), P(("dp", "pack"), None), P(("dp", "pack"), None), P()),
        check_vma=False,
    )
```

```python
import functools
import itertools
import math

import jax
import jax.numpy as jnp
from jax import lax
from jax.experimental import pallas as pl
from jax.experimental.pallas import tpu as pltpu
from jax.sharding import PartitionSpec as P

HEAD_DIM = 64
PAIR = 2 * HEAD_DIM
EX_DEV = 2
GROUPS = 16
CHUNKS = (1, 1)
LOCKSTEP = 4
ALONE = pltpu.CompilerParams(vmem_limit_bytes=60 * 1024 * 1024)
ROOM = pltpu.CompilerParams(vmem_limit_bytes=16 * 1024 * 1024)
FIELDS = 8
SMALL = pl.CostEstimate(flops=0, bytes_accessed=2 * 1024 * 1024, transcendentals=0)
ANY = pl.BlockSpec(memory_space=pl.ANY)
HBM = pl.BlockSpec(memory_space=pltpu.HBM)
SMEM = pl.BlockSpec(memory_space=pltpu.SMEM)
VMEM = pl.BlockSpec(memory_space=pltpu.VMEM)


def table_kernel(
    me_ref,
    input_ref,
    target_ref,
    enc_ref,
    dec_ref,
    task_ref,
    k_ref,
    v_ref,
    *refs,
):
    kv_ref, table_ref, count_ref, held, sem = refs[-5:]
    me = me_ref[0]
    core = lax.rem(me, 2)
    half = held.shape[-1]
    columns = pl.ds(pl.multiple_of((1 - core) * half, half), half)
    into = [
        pltpu.make_async_copy(source.at[:, columns], held.at[tensor], sem.at[tensor])
        for tensor, source in enumerate((k_ref, v_ref))
    ]
    out = [
        pltpu.make_async_copy(held.at[tensor], kv_ref.at[tensor], sem.at[2 + tensor])
        for tensor in range(2)
    ]
    for copy in into:
        copy.start()
    total = enc_ref.shape[1]
    for side in range(2):
        pack = me + side * (1 - 2 * core)

        def find(item, carry, pack=pack):
            first, second = carry
            hit = enc_ref[0, item] == pack
            return (
                jnp.where(hit & (first < 0), item, first),
                jnp.where(hit & (first >= 0), item, second),
            )

        first, second = lax.fori_loop(0, total, find, (jnp.int32(-1), jnp.int32(-1)))
        second = jnp.maximum(second, 0)
        first = jnp.maximum(first, 0)
        for place, item in enumerate((first, second)):
            row = 2 * side + place
            dec = dec_ref[0, item]

            def before(other, offset, dec=dec):
                return offset + jnp.where(dec_ref[0, other] == dec, target_ref[0, other], 0)

            table_ref[row, 0] = dec ^ me
            table_ref[row, 1] = lax.fori_loop(0, item, before, jnp.int32(0))
            table_ref[row, 2] = target_ref[0, item]
            table_ref[row, 3] = jnp.int32(0) if place == 0 else input_ref[0, first]
            table_ref[row, 4] = input_ref[0, item]
            table_ref[row, 5] = task_ref[0, item]
            table_ref[row, 6] = 0
            table_ref[row, 7] = 0
    lane = lax.broadcasted_iota(jnp.int32, (1, 128), 1)
    counts = jnp.zeros((1, 128), jnp.float32)
    for item in range(total):
        amount = target_ref[0, item].astype(jnp.float32)
        counts = counts + jnp.where(lane == task_ref[0, item], amount, 0.0)
    count_ref[...] = counts
    for tensor in range(2):
        into[tensor].wait()
        out[tensor].start()
    for tensor in range(2):
        out[tensor].wait()


def tabulate(me, lengths, targets, enc_pack, dec_pack, task, keys, values):
    rows, features = keys.shape
    half = features // 2
    return pl.pallas_call(
        table_kernel,
        out_shape=[
            jax.ShapeDtypeStruct((2, rows, half), keys.dtype),
            jax.ShapeDtypeStruct((4, FIELDS), jnp.int32),
            jax.ShapeDtypeStruct((1, 128), jnp.float32),
        ],
        in_specs=[SMEM] * 6 + [HBM] * 2,
        out_specs=[ANY, SMEM, VMEM],
        scratch_shapes=[pltpu.VMEM((2, rows, half), keys.dtype), pltpu.SemaphoreType.DMA((4,))],
        compiler_params=ROOM,
        cost_estimate=SMALL,
        name="tabulate",
    )(me, lengths, targets, enc_pack, dec_pack, task, keys, values)


def split_kernel(me_ref, q_ref, c_ref, own_ref, other_ref, held, sem):
    half = held.shape[-1]
    core = lax.rem(me_ref[0], 2)
    into, out = [], []
    for side, (base, target) in enumerate(((core, own_ref), (1 - core, other_ref))):
        columns = pl.ds(pl.multiple_of(base * half, PAIR), half)
        for tensor, source in enumerate((q_ref, c_ref)):
            place = 2 * side + tensor
            into.append(
                pltpu.make_async_copy(source.at[:, columns], held.at[place], sem.at[place])
            )
            out.append(
                pltpu.make_async_copy(held.at[place], target.at[tensor], sem.at[4 + place])
            )
    for copy in into:
        copy.start()
    for place in range(4):
        into[place].wait()
        out[place].start()
    for copy in out:
        copy.wait()


def split(me, queries, cotangent):
    rows, features = queries.shape
    half = features // 2
    return pl.pallas_call(
        split_kernel,
        out_shape=[jax.ShapeDtypeStruct((2, rows, half), queries.dtype)] * 2,
        in_specs=[SMEM] + [HBM] * 2,
        out_specs=[ANY] * 2,
        scratch_shapes=[
            pltpu.VMEM((4, rows, half), queries.dtype),
            pltpu.SemaphoreType.DMA((8,)),
        ],
        compiler_params=ROOM,
        cost_estimate=SMALL,
        name="split_columns",
    )(me, queries, cotangent)


def attention_kernel(
    me_ref, table_ref, scale_ref, *refs, packs, first, bases, half, at
):
    pieces = refs[:packs]
    k_ref, v_ref, sibling_ref = refs[packs : packs + 3]
    outs = refs[packs + 3 + (0 if first else 3) :]
    k_out, v_out, sibling_out = outs[:3]
    query_outs = outs[3 : 2 + packs]
    loss_out = outs[2 + packs]
    kv, qc, dq, dkv, loss, scaling, in_sem, qc_sem, out_sem, dkv_sem = outs[packs + 3 :]
    width = qc.shape[-1]
    rows = qc.shape[2]
    keys = kv.shape[2]
    core = lax.rem(me_ref[0], 2)
    own_columns = pl.ds(pl.multiple_of(core * half + at, PAIR), width)
    half_columns = pl.ds(at, width)
    kv_copies = [
        [
            pltpu.make_async_copy(k_ref.at[:, own_columns], kv.at[0, 0], in_sem.at[0, 0]),
            pltpu.make_async_copy(v_ref.at[:, own_columns], kv.at[0, 1], in_sem.at[0, 1]),
        ],
        [
            pltpu.make_async_copy(
                sibling_ref.at[tensor, :, half_columns], kv.at[1, tensor], in_sem.at[1, tensor]
            )
            for tensor in range(2)
        ],
    ]
    dkv_copies = [
        [
            pltpu.make_async_copy(dkv.at[0, 0], k_out.at[:, own_columns], dkv_sem.at[0, 0]),
            pltpu.make_async_copy(dkv.at[0, 1], v_out.at[:, own_columns], dkv_sem.at[0, 1]),
        ],
        [
            pltpu.make_async_copy(
                dkv.at[1, tensor],
                sibling_out.at[pl.ds(tensor * keys, keys), half_columns],
                dkv_sem.at[1, tensor],
            )
            for tensor in range(2)
        ],
    ]
    for side in range(2):
        for copy in kv_copies[side]:
            copy.start()
        for place in range(2):
            item = 2 * side + place
            owner = table_ref[item, 0]
            for distance, piece in enumerate(pieces):

                @pl.when(owner == distance)
                def _(piece=piece, item=item, distance=distance):
                    pltpu.make_async_copy(
                        piece.at[:, :, pl.ds(at - bases[distance], width)],
                        qc.at[item],
                        qc_sem.at[item],
                    ).start()

    dq[...] = jnp.zeros_like(dq)
    loss[...] = jnp.zeros_like(loss)
    lane = lax.broadcasted_iota(jnp.int32, (1, PAIR), 1)
    low = lane < HEAD_DIM
    row = lax.broadcasted_iota(jnp.int32, (rows, PAIR), 0)
    row_lane = lax.broadcasted_iota(jnp.int32, (1, rows), 1)
    key = lax.broadcasted_iota(jnp.int32, (keys, 1), 0)
    key_lane = lax.broadcasted_iota(jnp.int32, (1, keys), 1)

    def dot(left, right):
        return jnp.dot(left, right, preferred_element_type=jnp.float32)

    vector = jnp.zeros((1, 128), jnp.float32)
    for side in range(2):
        for copy in kv_copies[side]:
            copy.wait()
        for place in range(2):
            item = 2 * side + place
            pltpu.make_async_copy(
                pieces[0].at[:, :, half_columns], qc.at[item], qc_sem.at[item]
            ).wait()
        owner, scale_rows = [], []
        border = table_ref[2 * side, 4]
        for place in range(2):
            item = 2 * side + place
            start, length = table_ref[item, 1], table_ref[item, 2]
            scale = scale_ref[0, table_ref[item, 5]]
            scaling[place] = jnp.where((row >= start) & (row < start + length), scale, 0.0)
            scale_rows.append(
                jnp.where((row_lane >= start) & (row_lane < start + length), scale, 0.0)
            )
            owner.append(table_ref[item, 0])

        def pair_chain(pair, side=side, owner=owner, scale_rows=scale_rows, border=border):
            columns = pl.ds(pl.multiple_of(pair * PAIR, PAIR), PAIR)
            early, early_lane = key < border, key_lane < border
            key_pair = kv[side, 0, :, columns]
            value_pair = kv[side, 1, :, columns]
            zero = jnp.zeros_like(key_pair)
            blank = jnp.zeros((HEAD_DIM, rows), key_pair.dtype)

            def by_example(array):
                return jnp.concatenate(
                    [jnp.where(early, array, zero), jnp.where(early, zero, array)], axis=1
                )

            def by_head(array):
                nothing = jnp.zeros_like(array)
                return jnp.concatenate(
                    [jnp.where(low, array, nothing), jnp.where(low, nothing, array)], axis=0
                )

            def spread(turned):
                blocks = []
                for array in turned:
                    blocks.append(jnp.concatenate([array[:HEAD_DIM], blank], axis=1))
                    blocks.append(jnp.concatenate([blank, array[HEAD_DIM:]], axis=1))
                return jnp.concatenate(blocks, axis=0)

            def example_parts(turned, part):
                array = turned[part]
                nothing = jnp.zeros_like(array)
                return jnp.concatenate(
                    [jnp.where(early_lane, array, nothing), jnp.where(early_lane, nothing, array)],
                    axis=0,
                )

            queries = [qc[2 * side + place, 0, :, columns] for place in range(2)]
            cots = [qc[2 * side + place, 1, :, columns] for place in range(2)]
            yield
            ups = [
                (cots[place].astype(jnp.float32) * scaling[place]).astype(jnp.bfloat16)
                for place in range(2)
            ]
            key_turned, value_turned = key_pair.T, value_pair.T
            cots_turned = [cot.T.astype(jnp.float32) for cot in cots]
            ups_turned = [
                (cots_turned[place] * scale_rows[place]).astype(jnp.bfloat16) for place in range(2)
            ]
            queries_turned = [query.T for query in queries]
            yield
            scores = dot(by_example(key_pair), spread(queries_turned))
            slopes = dot(by_example(value_pair), spread(ups_turned))
            yield
            lowest = jnp.float32(-3e38)
            highest = [
                jnp.max(jnp.where(early, scores, lowest), axis=0, keepdims=True),
                jnp.max(jnp.where(early, lowest, scores), axis=0, keepdims=True),
            ]
            yield
            powers = jnp.exp(scores - jnp.where(early, highest[0], highest[1]))
            inverse = [
                1.0 / jnp.sum(jnp.where(early, powers, 0.0), axis=0, keepdims=True),
                1.0 / jnp.sum(jnp.where(early, 0.0, powers), axis=0, keepdims=True),
            ]
            yield
            weights = powers * jnp.where(early, inverse[0], inverse[1])
            weights_low = weights.astype(jnp.bfloat16)
            yield
            drifts = [[], []]
            losses = []
            for head in range(2):
                part = slice(head * HEAD_DIM, (head + 1) * HEAD_DIM)
                lanes = slice(head * rows, (head + 1) * rows)
                attended = dot(example_parts(value_turned, part), weights_low[:, lanes])
                attended = attended.astype(jnp.bfloat16).astype(jnp.float32)
                for place in range(2):
                    item = 2 * side + place
                    here = attended[place * HEAD_DIM : (place + 1) * HEAD_DIM]
                    token = cots_turned[place][part] * here
                    losses.append(
                        (item, jnp.sum(token.reshape(HEAD_DIM // 8, 8, rows), axis=0))
                    )
                    drifts[place].append(
                        jnp.sum(
                            ups_turned[place][part].astype(jnp.float32) * here,
                            axis=0,
                            keepdims=True,
                        )
                    )
            yield
            drift = [jnp.concatenate(parts, axis=1) for parts in drifts]
            grad = weights * (slopes - jnp.where(early, drift[0], drift[1]))
            grad = grad.astype(jnp.bfloat16)
            yield
            query_parts = [[], []]
            for head in range(2):
                part = slice(head * HEAD_DIM, (head + 1) * HEAD_DIM)
                lanes = slice(head * rows, (head + 1) * rows)
                found = dot(example_parts(key_turned, part), grad[:, lanes])
                for place in range(2):
                    query_parts[place].append(found[place * HEAD_DIM : (place + 1) * HEAD_DIM])
            key_grad = dot(grad, jnp.concatenate([by_head(query) for query in queries], axis=1))
            value_grad = dot(weights_low, jnp.concatenate([by_head(up) for up in ups], axis=1))
            yield
            query_grads = [
                jnp.concatenate(query_parts[place], axis=0).astype(jnp.bfloat16).T
                for place in range(2)
            ]
            pair_grads = [
                jnp.where(early, found[:, :PAIR], found[:, PAIR:]).astype(jnp.bfloat16)
                for found in (key_grad, value_grad)
            ]
            yield
            for place in range(2):
                at = owner[place]
                dq[at, :, columns] = dq[at, :, columns] + query_grads[place]
            for tensor in range(2):
                dkv[side, tensor, :, columns] = pair_grads[tensor]
            for item, part in losses:
                loss[item] += part

        def group_step(group, carry, pair_chain=pair_chain):
            chains = [pair_chain(group * lockstep + i) for i in range(lockstep)]
            for _ in itertools.zip_longest(*chains):
                pass
            return carry

        lockstep = math.gcd(LOCKSTEP, width // PAIR)
        lax.fori_loop(0, width // PAIR // lockstep, group_step, 0)
        for copy in dkv_copies[side]:
            copy.start()
        for place in range(2):
            item = 2 * side + place
            start, length = table_ref[item, 1], table_ref[item, 2]
            part = jnp.sum(loss[item], axis=0, keepdims=True)
            part = jnp.where((row_lane >= start) & (row_lane < start + length), part, 0.0)
            amount = jnp.sum(part, axis=1, keepdims=True)
            vector = vector + jnp.where(lane == table_ref[item, 5], amount, 0.0)

    targets = [query_outs[0], sibling_out.at[pl.ds(2 * keys, rows), half_columns], *query_outs[1:]]
    query_copies = [
        pltpu.make_async_copy(dq.at[distance], target, out_sem.at[distance])
        for distance, target in enumerate(targets)
    ]
    for copy in query_copies:
        copy.start()
    loss_out[...] = vector
    for side in range(2):
        for copy in dkv_copies[side]:
            copy.wait()
    for copy in query_copies:
        copy.wait()


def attention_chunk(
    me, table, scales, pieces, keys, values, sibling, full, packs, bases, at, width
):
    rows = pieces[0].shape[1]
    key_rows, features = keys.shape
    half = features // 2
    low = jnp.bfloat16
    first = full is None
    flops = rows * key_rows * width
    before = 3 + packs + 3
    return pl.pallas_call(
        functools.partial(
            attention_kernel,
            packs=packs,
            first=first,
            bases=bases,
            half=half,
            at=at,
        ),
        out_shape=[
            jax.ShapeDtypeStruct(keys.shape, low),
            jax.ShapeDtypeStruct(keys.shape, low),
            jax.ShapeDtypeStruct((2 * key_rows + rows, half), low),
        ]
        + [jax.ShapeDtypeStruct((rows, width), low)] * (packs - 1)
        + [jax.ShapeDtypeStruct((1, 128), jnp.float32)],
        in_specs=[SMEM] * 3 + [ANY] * packs + [HBM] * 2 + [ANY] + [HBM] * (0 if first else 3),
        out_specs=[HBM] * 3 + [ANY] * (packs - 1) + [VMEM],
        scratch_shapes=[
            pltpu.VMEM((2, 2, key_rows, width), low),
            pltpu.VMEM((4, 2, rows, width), low),
            pltpu.VMEM((packs, rows, width), low),
            pltpu.VMEM((2, 2, key_rows, width), low),
            pltpu.VMEM((4, 8, rows), jnp.float32),
            pltpu.VMEM((2, rows, PAIR), jnp.float32),
            pltpu.SemaphoreType.DMA((2, 2)),
            pltpu.SemaphoreType.DMA((4,)),
            pltpu.SemaphoreType.DMA((packs,)),
            pltpu.SemaphoreType.DMA((2, 2)),
        ],
        input_output_aliases={} if first else {before + i: i for i in range(3)},
        compiler_params=pltpu.CompilerParams(
            vmem_limit_bytes=14 * 1024 * 1024 + 2 * packs * rows * width
        ),
        cost_estimate=pl.CostEstimate(
            flops=flops, bytes_accessed=8 * 1024 * 1024, transcendentals=0
        ),
        name="attention_chunk",
    )(me, table, scales, *pieces, keys, values, sibling, *(() if first else full))


def finish_kernel(me_ref, *refs, counts, starts, half):
    back = refs[sum(counts)]
    outs = refs[sum(counts) + 3 : sum(counts) + 6]
    *merged, sem = refs[sum(counts) + 6 :]
    rows, keys = merged[0].shape[1], outs[1].shape[0]
    core = lax.rem(me_ref[0], 2)
    copies = []

    def write(source, out, columns):
        copies.append(pltpu.make_async_copy(source, out.at[:, columns], sem.at[len(copies)]))
        copies[-1].start()

    other = pl.ds(pl.multiple_of((1 - core) * half, PAIR), half)
    for tensor in range(2):
        write(back.at[pl.ds(tensor * keys, keys)], outs[1 + tensor], other)
    given = list(refs[: sum(counts)])
    for chunk, (at, held) in enumerate(zip(starts, merged)):
        width = held.shape[-1]
        for side, base in enumerate((core, 1 - core)):
            terms = [given.pop(0)[...] for _ in range(counts[2 * chunk + side])]
            if side == 1:
                terms.append(back[2 * keys : 2 * keys + rows, at : at + width])
            held[side] = functools.reduce(jnp.add, terms)
            columns = pl.ds(pl.multiple_of(base * half + at, PAIR), width)
            write(held.at[side], outs[0], columns)
    for copy in copies:
        copy.wait()


def finish(me, ends, starts, packs, back, like, keys, values):
    parts = [part for near, far in ends for part in near + far]
    counts = [len(side) for end in ends for side in end]
    return pl.pallas_call(
        functools.partial(
            finish_kernel, counts=counts, starts=starts, half=like.shape[1] // 2
        ),
        out_shape=[
            jax.ShapeDtypeStruct(array.shape, array.dtype) for array in (like, keys, values)
        ],
        in_specs=[SMEM] + [VMEM] * (len(parts) + 1) + [HBM] * 2,
        out_specs=[HBM] * 3,
        scratch_shapes=[pltpu.VMEM((2, *near[0].shape), like.dtype) for near, _ in ends]
        + [pltpu.SemaphoreType.DMA((2 + 2 * len(ends),))],
        input_output_aliases={len(parts) + 2: 1, len(parts) + 3: 2},
        compiler_params=pltpu.CompilerParams(vmem_limit_bytes=(8 + packs) * 1024 * 1024),
        cost_estimate=SMALL,
        name="finish",
    )(me, *parts, back, keys, values)


def swap(array, axis_name, size, bits):
    return lax.ppermute(array, axis_name, [(i, i ^ bits) for i in range(size)])


def doubled_sum(array, axis_name, size, first=1, last=None):
    step = first
    while step < (last or size):
        array = array + swap(array, axis_name, size, step)
        step *= 2
    return array


together = lax.optimization_barrier


def local(
    enc_keys,
    enc_values,
    dec_queries,
    cotangent,
    input_lengths,
    target_lengths,
    enc_pack,
    dec_pack,
    task_group,
    dro_weights,
    *,
    packs,
    groups,
):
    me = lax.axis_index("pack").astype(jnp.int32).reshape(1)
    rows, features = dec_queries.shape
    half = features // 2
    total_tokens = rows * packs * groups
    relayed = packs == 8

    def swapped(array, bits):
        return swap(array, "pack", packs, bits)

    def tabulated(me):
        return tabulate(
            me,
            input_lengths,
            target_lengths,
            enc_pack,
            dec_pack,
            task_group[:, :, 0],
            enc_keys,
            enc_values,
        )

    def scales_of(group_counts):
        counts = doubled_sum(group_counts, "dp", groups)
        weights = dro_weights.astype(jnp.float32)
        weights = jnp.pad(weights, (0, 128 - GROUPS)).reshape(1, 128)
        return counts, weights / jnp.sum(weights) * (total_tokens / counts)

    widths = [half * share // sum(CHUNKS) for share in CHUNKS]
    starts = [sum(widths[:i]) for i in range(len(widths))]
    spots = list(zip(starts, widths))
    own, other = split(me, dec_queries, cotangent)
    if not relayed:
        pieces = [own] + [swapped(other if i & 1 else own, i) for i in range(1, packs)]
        kv_other, table, group_counts = tabulated(me)
        kv_sibling = swapped(kv_other, 1)
        counts, scales = scales_of(group_counts)
        full, losses, ends = None, [], []
        for at, width in spots:
            *result, loss = attention_chunk(
                me, table, scales, pieces, enc_keys, enc_values, kv_sibling, full,
                packs, [0] * packs, at, width,
            )
            full, parts = result[:3], result[3:]
            losses.append(loss)
            arrived = [swapped(part, i) for i, part in enumerate(parts[1:], 2)]
            ends.append((parts[:1] + arrived[0::2], arrived[1::2]))
        back = swapped(full[2], 1)
        loss = doubled_sum(functools.reduce(jnp.add, losses), "pack", packs)
        loss = doubled_sum(loss, "dp", groups)
    else:
        first = widths[0]
        x_own, y_other = swapped(own, 2), swapped(other, 5)
        x_other, y_own = swapped(other, 3), swapped(own, 4)
        sibling = swapped(other, 1)
        x_own, y_other = together((x_own, y_other))
        near = [x_own[:, :, :first], x_own[:, :, first:]]
        far = [y_other[:, :, :first], y_other[:, :, first:]]
        diagonal = [swapped(near[0], 4), swapped(far[0], 2)]
        me_later, x_other = together((me, x_other))
        kv_other, table, group_counts = tabulated(me_later)
        kv_sibling = swapped(kv_other, 1)
        counts, scales = scales_of(group_counts)
        y_own, x_other, sibling, kv_sibling, scales, diagonal, near, far = together(
            (y_own, x_other, sibling, kv_sibling, scales, diagonal, near, far)
        )
        later = [swapped(near[1], 4), swapped(far[1], 2)]

        def attend(full, chunk, diagonal, base):
            at, width = spots[chunk]
            pieces = [own, sibling, x_own, x_other, y_own, y_other, *diagonal]
            *result, loss = attention_chunk(
                me, table, scales, pieces, enc_keys, enc_values, kv_sibling, full,
                packs, [0] * 6 + [base] * 2, at, width,
            )
            return result[:3], result[3:], loss

        def forwarded(parts):
            return [swapped(parts[5], 2), swapped(parts[6], 4)]

        def sent(parts):
            return [swapped(parts[1], 2), swapped(parts[4], 5)]

        def merged(parts, relay):
            return [swapped(parts[3] + relay[0], 4), swapped(parts[2] + relay[1], 3)]

        def sums(parts, direct, last):
            return [parts[0], direct[0], last[0]], [direct[1], last[1]]

        full, parts_a, loss_a = attend(None, 0, diagonal, 0)
        later, full, parts_a = together((later, full, parts_a))

        relay_a, direct_a = forwarded(parts_a), sent(parts_a)
        full, parts_b, loss_b = attend(full, 1, later, first)
        relay_a, direct_a, full, parts_b, loss_b = together(
            (relay_a, direct_a, full, parts_b, loss_b)
        )

        last_a, relay_b = merged(parts_a, relay_a), forwarded(parts_b)
        loss = doubled_sum(loss_a + loss_b, "dp", groups)
        loss = doubled_sum(loss, "pack", packs, 1, 2)
        last_a, relay_b, loss, full = together((last_a, relay_b, loss, full))

        last_b, direct_b = merged(parts_b, relay_b), sent(parts_b)
        back = swapped(full[2], 1)
        loss = doubled_sum(loss, "pack", packs, 2, 4)
        last_b, direct_b, back, loss = together((last_b, direct_b, back, loss))
        loss = doubled_sum(loss, "pack", packs, 4)
        ends = [sums(parts_a, direct_a, last_a), sums(parts_b, direct_b, last_b)]

    queries_gradient, keys_gradient, values_gradient = finish(
        me, ends, starts, packs, back, dec_queries, *full[:2]
    )
    group_loss = (loss / counts)[0, :GROUPS]
    return (queries_gradient, keys_gradient, values_gradient, group_loss)


def solution(mesh):
    placed = (
        P(("dp", "pack"), None),
        P(("dp", "pack"), None),
        P(("dp", "pack"), None),
        P(("dp", "pack"), None),
        P("dp", None),
        P("dp", None),
        P("dp", None),
        P("dp", None),
        P("dp", None, None),
        P(),
    )
    return jax.shard_map(
        functools.partial(local, packs=mesh.shape["pack"], groups=mesh.shape["dp"]),
        mesh=mesh,
        in_specs=placed,
        out_specs=(P(("dp", "pack"), None), P(("dp", "pack"), None), P(("dp", "pack"), None), P()),
        check_vma=False,
    )
```

```python
import functools
import itertools
import math

import jax
import jax.numpy as jnp
from jax import lax
from jax.experimental import pallas as pl
from jax.experimental.pallas import tpu as pltpu
from jax.sharding import PartitionSpec as P

HEAD_DIM = 64
PAIR = 2 * HEAD_DIM
EX_DEV = 2
GROUPS = 16
CHUNKS = (1, 1)
LOCKSTEP = 4
ALONE = pltpu.CompilerParams(vmem_limit_bytes=60 * 1024 * 1024)
ROOM = pltpu.CompilerParams(vmem_limit_bytes=16 * 1024 * 1024)
FIELDS = 8
SMALL = pl.CostEstimate(flops=0, bytes_accessed=2 * 1024 * 1024, transcendentals=0)
ANY = pl.BlockSpec(memory_space=pl.ANY)
HBM = pl.BlockSpec(memory_space=pltpu.HBM)
SMEM = pl.BlockSpec(memory_space=pltpu.SMEM)
VMEM = pl.BlockSpec(memory_space=pltpu.VMEM)


def table_kernel(
    me_ref,
    input_ref,
    target_ref,
    enc_ref,
    dec_ref,
    task_ref,
    k_ref,
    v_ref,
    *refs,
):
    kv_ref, table_ref, count_ref, held, sem = refs[-5:]
    me = me_ref[0]
    core = lax.rem(me, 2)
    half = held.shape[-1]
    columns = pl.ds(pl.multiple_of((1 - core) * half, half), half)
    into = [
        pltpu.make_async_copy(source.at[:, columns], held.at[tensor], sem.at[tensor])
        for tensor, source in enumerate((k_ref, v_ref))
    ]
    out = [
        pltpu.make_async_copy(held.at[tensor], kv_ref.at[tensor], sem.at[2 + tensor])
        for tensor in range(2)
    ]
    for copy in into:
        copy.start()
    total = enc_ref.shape[1]
    for side in range(2):
        pack = me + side * (1 - 2 * core)

        def find(item, carry, pack=pack):
            first, second = carry
            hit = enc_ref[0, item] == pack
            return (
                jnp.where(hit & (first < 0), item, first),
                jnp.where(hit & (first >= 0), item, second),
            )

        first, second = lax.fori_loop(0, total, find, (jnp.int32(-1), jnp.int32(-1)))
        second = jnp.maximum(second, 0)
        first = jnp.maximum(first, 0)
        for place, item in enumerate((first, second)):
            row = 2 * side + place
            dec = dec_ref[0, item]

            def before(other, offset, dec=dec):
                return offset + jnp.where(dec_ref[0, other] == dec, target_ref[0, other], 0)

            table_ref[row, 0] = dec ^ me
            table_ref[row, 1] = lax.fori_loop(0, item, before, jnp.int32(0))
            table_ref[row, 2] = target_ref[0, item]
            table_ref[row, 3] = jnp.int32(0) if place == 0 else input_ref[0, first]
            table_ref[row, 4] = input_ref[0, item]
            table_ref[row, 5] = task_ref[0, item]
            table_ref[row, 6] = 0
            table_ref[row, 7] = 0
    lane = lax.broadcasted_iota(jnp.int32, (1, 128), 1)
    counts = jnp.zeros((1, 128), jnp.float32)
    for item in range(total):
        amount = target_ref[0, item].astype(jnp.float32)
        counts = counts + jnp.where(lane == task_ref[0, item], amount, 0.0)
    count_ref[...] = counts
    for tensor in range(2):
        into[tensor].wait()
        out[tensor].start()
    for tensor in range(2):
        out[tensor].wait()


def tabulate(me, lengths, targets, enc_pack, dec_pack, task, keys, values):
    rows, features = keys.shape
    half = features // 2
    return pl.pallas_call(
        table_kernel,
        out_shape=[
            jax.ShapeDtypeStruct((2, rows, half), keys.dtype),
            jax.ShapeDtypeStruct((4, FIELDS), jnp.int32),
            jax.ShapeDtypeStruct((1, 128), jnp.float32),
        ],
        in_specs=[SMEM] * 6 + [HBM] * 2,
        out_specs=[ANY, SMEM, VMEM],
        scratch_shapes=[pltpu.VMEM((2, rows, half), keys.dtype), pltpu.SemaphoreType.DMA((4,))],
        compiler_params=ROOM,
        cost_estimate=SMALL,
        name="tabulate",
    )(me, lengths, targets, enc_pack, dec_pack, task, keys, values)


def split_kernel(me_ref, q_ref, c_ref, own_ref, other_ref, held, sem):
    half = held.shape[-1]
    core = lax.rem(me_ref[0], 2)
    into, out = [], []
    for side, (base, target) in enumerate(((core, own_ref), (1 - core, other_ref))):
        columns = pl.ds(pl.multiple_of(base * half, PAIR), half)
        for tensor, source in enumerate((q_ref, c_ref)):
            place = 2 * side + tensor
            into.append(
                pltpu.make_async_copy(source.at[:, columns], held.at[place], sem.at[place])
            )
            out.append(
                pltpu.make_async_copy(held.at[place], target.at[tensor], sem.at[4 + place])
            )
    for copy in into:
        copy.start()
    for place in range(4):
        into[place].wait()
        out[place].start()
    for copy in out:
        copy.wait()


def split(me, queries, cotangent):
    rows, features = queries.shape
    half = features // 2
    return pl.pallas_call(
        split_kernel,
        out_shape=[jax.ShapeDtypeStruct((2, rows, half), queries.dtype)] * 2,
        in_specs=[SMEM] + [HBM] * 2,
        out_specs=[ANY] * 2,
        scratch_shapes=[
            pltpu.VMEM((4, rows, half), queries.dtype),
            pltpu.SemaphoreType.DMA((8,)),
        ],
        compiler_params=ROOM,
        cost_estimate=SMALL,
        name="split_columns",
    )(me, queries, cotangent)


def attention_kernel(
    me_ref, table_ref, scale_ref, *refs, packs, first, bases, half, at
):
    pieces = refs[:packs]
    k_ref, v_ref, sibling_ref = refs[packs : packs + 3]
    outs = refs[packs + 3 + (0 if first else 3) :]
    k_out, v_out, sibling_out = outs[:3]
    query_outs = outs[3 : 2 + packs]
    loss_out = outs[2 + packs]
    kv, qc, dq, dkv, loss, scaling, in_sem, qc_sem, out_sem, dkv_sem = outs[packs + 3 :]
    width = qc.shape[-1]
    rows = qc.shape[2]
    keys = kv.shape[2]
    core = lax.rem(me_ref[0], 2)
    own_columns = pl.ds(pl.multiple_of(core * half + at, PAIR), width)
    half_columns = pl.ds(at, width)
    kv_copies = [
        [
            pltpu.make_async_copy(k_ref.at[:, own_columns], kv.at[0, 0], in_sem.at[0, 0]),
            pltpu.make_async_copy(v_ref.at[:, own_columns], kv.at[0, 1], in_sem.at[0, 1]),
        ],
        [
            pltpu.make_async_copy(
                sibling_ref.at[tensor, :, half_columns], kv.at[1, tensor], in_sem.at[1, tensor]
            )
            for tensor in range(2)
        ],
    ]
    dkv_copies = [
        [
            pltpu.make_async_copy(dkv.at[0, 0], k_out.at[:, own_columns], dkv_sem.at[0, 0]),
            pltpu.make_async_copy(dkv.at[0, 1], v_out.at[:, own_columns], dkv_sem.at[0, 1]),
        ],
        [
            pltpu.make_async_copy(
                dkv.at[1, tensor],
                sibling_out.at[pl.ds(tensor * keys, keys), half_columns],
                dkv_sem.at[1, tensor],
            )
            for tensor in range(2)
        ],
    ]
    for side in range(2):
        for copy in kv_copies[side]:
            copy.start()
        for place in range(2):
            item = 2 * side + place
            owner = table_ref[item, 0]
            for distance, piece in enumerate(pieces):

                @pl.when(owner == distance)
                def _(piece=piece, item=item, distance=distance):
                    pltpu.make_async_copy(
                        piece.at[:, :, pl.ds(at - bases[distance], width)],
                        qc.at[item],
                        qc_sem.at[item],
                    ).start()

    dq[...] = jnp.zeros_like(dq)
    loss[...] = jnp.zeros_like(loss)
    lane = lax.broadcasted_iota(jnp.int32, (1, PAIR), 1)
    low = lane < HEAD_DIM
    row = lax.broadcasted_iota(jnp.int32, (rows, PAIR), 0)
    row_lane = lax.broadcasted_iota(jnp.int32, (1, rows), 1)
    key = lax.broadcasted_iota(jnp.int32, (keys, 1), 0)
    key_lane = lax.broadcasted_iota(jnp.int32, (1, keys), 1)

    def dot(left, right):
        return jnp.dot(left, right, preferred_element_type=jnp.float32)

    vector = jnp.zeros((1, 128), jnp.float32)
    for side in range(2):
        for copy in kv_copies[side]:
            copy.wait()
        for place in range(2):
            item = 2 * side + place
            pltpu.make_async_copy(
                pieces[0].at[:, :, half_columns], qc.at[item], qc_sem.at[item]
            ).wait()
        owner, scale_rows = [], []
        border = table_ref[2 * side, 4]
        for place in range(2):
            item = 2 * side + place
            start, length = table_ref[item, 1], table_ref[item, 2]
            scale = scale_ref[0, table_ref[item, 5]]
            scaling[place] = jnp.where((row >= start) & (row < start + length), scale, 0.0)
            scale_rows.append(
                jnp.where((row_lane >= start) & (row_lane < start + length), scale, 0.0)
            )
            owner.append(table_ref[item, 0])

        def pair_chain(pair, side=side, owner=owner, scale_rows=scale_rows, border=border):
            columns = pl.ds(pl.multiple_of(pair * PAIR, PAIR), PAIR)
            early, early_lane = key < border, key_lane < border
            key_pair = kv[side, 0, :, columns]
            value_pair = kv[side, 1, :, columns]
            zero = jnp.zeros_like(key_pair)
            blank = jnp.zeros((HEAD_DIM, rows), key_pair.dtype)

            def by_example(array):
                return jnp.concatenate(
                    [jnp.where(early, array, zero), jnp.where(early, zero, array)], axis=1
                )

            def by_head(array):
                nothing = jnp.zeros_like(array)
                return jnp.concatenate(
                    [jnp.where(low, array, nothing), jnp.where(low, nothing, array)], axis=0
                )

            def spread(turned):
                blocks = []
                for array in turned:
                    blocks.append(jnp.concatenate([array[:HEAD_DIM], blank], axis=1))
                    blocks.append(jnp.concatenate([blank, array[HEAD_DIM:]], axis=1))
                return jnp.concatenate(blocks, axis=0)

            def example_parts(turned, part):
                array = turned[part]
                nothing = jnp.zeros_like(array)
                return jnp.concatenate(
                    [jnp.where(early_lane, array, nothing), jnp.where(early_lane, nothing, array)],
                    axis=0,
                )

            queries = [qc[2 * side + place, 0, :, columns] for place in range(2)]
            cots = [qc[2 * side + place, 1, :, columns] for place in range(2)]
            yield
            ups = [
                (cots[place].astype(jnp.float32) * scaling[place]).astype(jnp.bfloat16)
                for place in range(2)
            ]
            key_turned, value_turned = key_pair.T, value_pair.T
            cots_turned = [cot.T.astype(jnp.float32) for cot in cots]
            ups_turned = [
                (cots_turned[place] * scale_rows[place]).astype(jnp.bfloat16) for place in range(2)
            ]
            queries_turned = [query.T for query in queries]
            yield
            scores = dot(by_example(key_pair), spread(queries_turned))
            slopes = dot(by_example(value_pair), spread(ups_turned))
            yield
            lowest = jnp.float32(-3e38)
            highest = [
                jnp.max(jnp.where(early, scores, lowest), axis=0, keepdims=True),
                jnp.max(jnp.where(early, lowest, scores), axis=0, keepdims=True),
            ]
            yield
            powers = jnp.exp(scores - jnp.where(early, highest[0], highest[1]))
            inverse = [
                1.0 / jnp.sum(jnp.where(early, powers, 0.0), axis=0, keepdims=True),
                1.0 / jnp.sum(jnp.where(early, 0.0, powers), axis=0, keepdims=True),
            ]
            yield
            weights = powers * jnp.where(early, inverse[0], inverse[1])
            weights_low = weights.astype(jnp.bfloat16)
            yield
            drifts = [[], []]
            losses = []
            for head in range(2):
                part = slice(head * HEAD_DIM, (head + 1) * HEAD_DIM)
                lanes = slice(head * rows, (head + 1) * rows)
                attended = dot(example_parts(value_turned, part), weights_low[:, lanes])
                attended = attended.astype(jnp.bfloat16).astype(jnp.float32)
                for place in range(2):
                    item = 2 * side + place
                    here = attended[place * HEAD_DIM : (place + 1) * HEAD_DIM]
                    token = cots_turned[place][part] * here
                    losses.append(
                        (item, jnp.sum(token.reshape(HEAD_DIM // 8, 8, rows), axis=0))
                    )
                    drifts[place].append(
                        jnp.sum(
                            ups_turned[place][part].astype(jnp.float32) * here,
                            axis=0,
                            keepdims=True,
                        )
                    )
            yield
            drift = [jnp.concatenate(parts, axis=1) for parts in drifts]
            grad = weights * (slopes - jnp.where(early, drift[0], drift[1]))
            grad = grad.astype(jnp.bfloat16)
            yield
            query_parts = [[], []]
            for head in range(2):
                part = slice(head * HEAD_DIM, (head + 1) * HEAD_DIM)
                lanes = slice(head * rows, (head + 1) * rows)
                found = dot(example_parts(key_turned, part), grad[:, lanes])
                for place in range(2):
                    query_parts[place].append(found[place * HEAD_DIM : (place + 1) * HEAD_DIM])
            key_grad = dot(grad, jnp.concatenate([by_head(query) for query in queries], axis=1))
            value_grad = dot(weights_low, jnp.concatenate([by_head(up) for up in ups], axis=1))
            yield
            query_grads = [
                jnp.concatenate(query_parts[place], axis=0).astype(jnp.bfloat16).T
                for place in range(2)
            ]
            pair_grads = [
                jnp.where(early, found[:, :PAIR], found[:, PAIR:]).astype(jnp.bfloat16)
                for found in (key_grad, value_grad)
            ]
            yield
            for place in range(2):
                at = owner[place]
                dq[at, :, columns] = dq[at, :, columns] + query_grads[place]
            for tensor in range(2):
                dkv[side, tensor, :, columns] = pair_grads[tensor]
            for item, part in losses:
                loss[item] += part

        def group_step(group, carry, pair_chain=pair_chain):
            chains = [pair_chain(group * lockstep + i) for i in range(lockstep)]
            for _ in itertools.zip_longest(*chains):
                pass
            return carry

        lockstep = math.gcd(LOCKSTEP, width // PAIR)
        lax.fori_loop(0, width // PAIR // lockstep, group_step, 0)
        for copy in dkv_copies[side]:
            copy.start()
        for place in range(2):
            item = 2 * side + place
            start, length = table_ref[item, 1], table_ref[item, 2]
            part = jnp.sum(loss[item], axis=0, keepdims=True)
            part = jnp.where((row_lane >= start) & (row_lane < start + length), part, 0.0)
            amount = jnp.sum(part, axis=1, keepdims=True)
            vector = vector + jnp.where(lane == table_ref[item, 5], amount, 0.0)

    targets = [query_outs[0], sibling_out.at[pl.ds(2 * keys, rows), half_columns], *query_outs[1:]]
    query_copies = [
        pltpu.make_async_copy(dq.at[distance], target, out_sem.at[distance])
        for distance, target in enumerate(targets)
    ]
    for copy in query_copies:
        copy.start()
    loss_out[...] = vector
    for side in range(2):
        for copy in dkv_copies[side]:
            copy.wait()
    for copy in query_copies:
        copy.wait()


def attention_chunk(
    me, table, scales, pieces, keys, values, sibling, full, packs, bases, at, width
):
    rows = pieces[0].shape[1]
    key_rows, features = keys.shape
    half = features // 2
    low = jnp.bfloat16
    first = full is None
    flops = rows * key_rows * width
    before = 3 + packs + 3
    return pl.pallas_call(
        functools.partial(
            attention_kernel,
            packs=packs,
            first=first,
            bases=bases,
            half=half,
            at=at,
        ),
        out_shape=[
            jax.ShapeDtypeStruct(keys.shape, low),
            jax.ShapeDtypeStruct(keys.shape, low),
            jax.ShapeDtypeStruct((2 * key_rows + rows, half), low),
        ]
        + [jax.ShapeDtypeStruct((rows, width), low)] * (packs - 1)
        + [jax.ShapeDtypeStruct((1, 128), jnp.float32)],
        in_specs=[SMEM] * 3 + [ANY] * packs + [HBM] * 2 + [ANY] + [HBM] * (0 if first else 3),
        out_specs=[HBM] * 3 + [ANY] * (packs - 1) + [VMEM],
        scratch_shapes=[
            pltpu.VMEM((2, 2, key_rows, width), low),
            pltpu.VMEM((4, 2, rows, width), low),
            pltpu.VMEM((packs, rows, width), low),
            pltpu.VMEM((2, 2, key_rows, width), low),
            pltpu.VMEM((4, 8, rows), jnp.float32),
            pltpu.VMEM((2, rows, PAIR), jnp.float32),
            pltpu.SemaphoreType.DMA((2, 2)),
            pltpu.SemaphoreType.DMA((4,)),
            pltpu.SemaphoreType.DMA((packs,)),
            pltpu.SemaphoreType.DMA((2, 2)),
        ],
        input_output_aliases={} if first else {before + i: i for i in range(3)},
        compiler_params=pltpu.CompilerParams(
            vmem_limit_bytes=14 * 1024 * 1024 + 2 * packs * rows * width
        ),
        cost_estimate=pl.CostEstimate(
            flops=flops, bytes_accessed=8 * 1024 * 1024, transcendentals=0
        ),
        name="attention_chunk",
    )(me, table, scales, *pieces, keys, values, sibling, *(() if first else full))


def finish_kernel(me_ref, *refs, counts, starts, half):
    back = refs[sum(counts)]
    outs = refs[sum(counts) + 3 : sum(counts) + 6]
    *merged, sem = refs[sum(counts) + 6 :]
    rows, keys = merged[0].shape[1], outs[1].shape[0]
    core = lax.rem(me_ref[0], 2)
    copies = []

    def write(source, out, columns):
        copies.append(pltpu.make_async_copy(source, out.at[:, columns], sem.at[len(copies)]))
        copies[-1].start()

    other = pl.ds(pl.multiple_of((1 - core) * half, PAIR), half)
    for tensor in range(2):
        write(back.at[pl.ds(tensor * keys, keys)], outs[1 + tensor], other)
    given = list(refs[: sum(counts)])
    for chunk, (at, held) in enumerate(zip(starts, merged)):
        width = held.shape[-1]
        for side, base in enumerate((core, 1 - core)):
            terms = [given.pop(0)[...] for _ in range(counts[2 * chunk + side])]
            if side == 1:
                terms.append(back[2 * keys : 2 * keys + rows, at : at + width])
            held[side] = functools.reduce(jnp.add, terms)
            columns = pl.ds(pl.multiple_of(base * half + at, PAIR), width)
            write(held.at[side], outs[0], columns)
    for copy in copies:
        copy.wait()


def finish(me, ends, starts, packs, back, like, keys, values):
    parts = [part for near, far in ends for part in near + far]
    counts = [len(side) for end in ends for side in end]
    return pl.pallas_call(
        functools.partial(
            finish_kernel, counts=counts, starts=starts, half=like.shape[1] // 2
        ),
        out_shape=[
            jax.ShapeDtypeStruct(array.shape, array.dtype) for array in (like, keys, values)
        ],
        in_specs=[SMEM] + [VMEM] * (len(parts) + 1) + [HBM] * 2,
        out_specs=[HBM] * 3,
        scratch_shapes=[pltpu.VMEM((2, *near[0].shape), like.dtype) for near, _ in ends]
        + [pltpu.SemaphoreType.DMA((2 + 2 * len(ends),))],
        input_output_aliases={len(parts) + 2: 1, len(parts) + 3: 2},
        compiler_params=pltpu.CompilerParams(vmem_limit_bytes=(8 + packs) * 1024 * 1024),
        cost_estimate=SMALL,
        name="finish",
    )(me, *parts, back, keys, values)


def swap(array, axis_name, size, bits):
    return lax.ppermute(array, axis_name, [(i, i ^ bits) for i in range(size)])


def doubled_sum(array, axis_name, size, first=1, last=None):
    step = first
    while step < (last or size):
        array = array + swap(array, axis_name, size, step)
        step *= 2
    return array


together = lax.optimization_barrier


def local(
    enc_keys,
    enc_values,
    dec_queries,
    cotangent,
    input_lengths,
    target_lengths,
    enc_pack,
    dec_pack,
    task_group,
    dro_weights,
    *,
    packs,
    groups,
):
    me = lax.axis_index("pack").astype(jnp.int32).reshape(1)
    rows, features = dec_queries.shape
    half = features // 2
    total_tokens = rows * packs * groups
    relayed = packs == 8

    def swapped(array, bits):
        return swap(array, "pack", packs, bits)

    def tabulated(me):
        return tabulate(
            me,
            input_lengths,
            target_lengths,
            enc_pack,
            dec_pack,
            task_group[:, :, 0],
            enc_keys,
            enc_values,
        )

    def scales_of(group_counts):
        counts = doubled_sum(group_counts, "dp", groups)
        weights = dro_weights.astype(jnp.float32)
        weights = jnp.pad(weights, (0, 128 - GROUPS)).reshape(1, 128)
        return counts, weights / jnp.sum(weights) * (total_tokens / counts)

    widths = [half * share // sum(CHUNKS) for share in CHUNKS]
    starts = [sum(widths[:i]) for i in range(len(widths))]
    spots = list(zip(starts, widths))
    own, other = split(me, dec_queries, cotangent)
    if not relayed:
        pieces = [own] + [swapped(other if i & 1 else own, i) for i in range(1, packs)]
        kv_other, table, group_counts = tabulated(me)
        kv_sibling = swapped(kv_other, 1)
        counts, scales = scales_of(group_counts)
        full, losses, ends = None, [], []
        for at, width in spots:
            *result, loss = attention_chunk(
                me, table, scales, pieces, enc_keys, enc_values, kv_sibling, full,
                packs, [0] * packs, at, width,
            )
            full, parts = result[:3], result[3:]
            losses.append(loss)
            arrived = [swapped(part, i) for i, part in enumerate(parts[1:], 2)]
            ends.append((parts[:1] + arrived[0::2], arrived[1::2]))
        back = swapped(full[2], 1)
        loss = doubled_sum(functools.reduce(jnp.add, losses), "pack", packs)
        loss = doubled_sum(loss, "dp", groups)
    else:
        first = widths[0]
        x_own, y_own = swapped(own, 2), swapped(own, 4)
        x_other, y_other = swapped(other, 3), swapped(other, 5)
        sibling = swapped(other, 1)
        me_later, x_own = together((me, x_own))
        kv_other, table, group_counts = tabulated(me_later)
        near = [x_own[:, :, :first], x_own[:, :, first:]]
        x_own, y_own, x_other, y_other, sibling, kv_other, group_counts, table, near = together(
            (x_own, y_own, x_other, y_other, sibling, kv_other, group_counts, table, near)
        )
        far = [y_other[:, :, :first], y_other[:, :, first:]]
        diagonal = [swapped(near[0], 4), swapped(far[0], 2)]
        kv_sibling = swapped(kv_other, 1)
        counts, scales = scales_of(group_counts)
        diagonal, near, far, kv_sibling, scales = together(
            (diagonal, near, far, kv_sibling, scales)
        )
        later = [swapped(near[1], 4), swapped(far[1], 2)]

        def attend(full, chunk, diagonal, base):
            at, width = spots[chunk]
            pieces = [own, sibling, x_own, x_other, y_own, y_other, *diagonal]
            *result, loss = attention_chunk(
                me, table, scales, pieces, enc_keys, enc_values, kv_sibling, full,
                packs, [0] * 6 + [base] * 2, at, width,
            )
            return result[:3], result[3:], loss

        def forwarded(parts):
            return [swapped(parts[5], 2), swapped(parts[6], 4)]

        def sent(parts):
            return [swapped(parts[1], 2), swapped(parts[4], 5)]

        def merged(parts, relay):
            return [swapped(parts[3] + relay[0], 4), swapped(parts[2] + relay[1], 3)]

        def sums(parts, direct, last):
            return [parts[0], direct[0], last[0]], [direct[1], last[1]]

        full, parts_a, loss_a = attend(None, 0, diagonal, 0)
        later, full, parts_a = together((later, full, parts_a))

        relay_a, direct_a = forwarded(parts_a), sent(parts_a)
        full, parts_b, loss_b = attend(full, 1, later, first)
        relay_a, direct_a, full, parts_b, loss_b = together(
            (relay_a, direct_a, full, parts_b, loss_b)
        )

        last_a, relay_b = merged(parts_a, relay_a), forwarded(parts_b)
        loss = doubled_sum(loss_a + loss_b, "dp", groups)
        loss = doubled_sum(loss, "pack", packs, 1, 2)
        last_a, relay_b, loss, full = together((last_a, relay_b, loss, full))

        last_b, direct_b = merged(parts_b, relay_b), sent(parts_b)
        back = swapped(full[2], 1)
        loss = doubled_sum(loss, "pack", packs, 2, 4)
        last_b, direct_b, back, loss = together((last_b, direct_b, back, loss))
        loss = doubled_sum(loss, "pack", packs, 4)
        ends = [sums(parts_a, direct_a, last_a), sums(parts_b, direct_b, last_b)]

    queries_gradient, keys_gradient, values_gradient = finish(
        me, ends, starts, packs, back, dec_queries, *full[:2]
    )
    group_loss = (loss / counts)[0, :GROUPS]
    return (queries_gradient, keys_gradient, values_gradient, group_loss)


def solution(mesh):
    placed = (
        P(("dp", "pack"), None),
        P(("dp", "pack"), None),
        P(("dp", "pack"), None),
        P(("dp", "pack"), None),
        P("dp", None),
        P("dp", None),
        P("dp", None),
        P("dp", None),
        P("dp", None, None),
        P(),
    )
    return jax.shard_map(
        functools.partial(local, packs=mesh.shape["pack"], groups=mesh.shape["dp"]),
        mesh=mesh,
        in_specs=placed,
        out_specs=(P(("dp", "pack"), None), P(("dp", "pack"), None), P(("dp", "pack"), None), P()),
        check_vma=False,
    )
```

```python
import functools
import itertools
import math

import jax
import jax.numpy as jnp
from jax import lax
from jax.experimental import pallas as pl
from jax.experimental.pallas import tpu as pltpu
from jax.sharding import PartitionSpec as P

HEAD_DIM = 64
PAIR = 2 * HEAD_DIM
EX_DEV = 2
GROUPS = 16
CHUNKS = (1, 1)
LOCKSTEP = 4
ALONE = pltpu.CompilerParams(vmem_limit_bytes=60 * 1024 * 1024)
ROOM = pltpu.CompilerParams(vmem_limit_bytes=16 * 1024 * 1024)
FIELDS = 8
SMALL = pl.CostEstimate(flops=0, bytes_accessed=2 * 1024 * 1024, transcendentals=0)
ANY = pl.BlockSpec(memory_space=pl.ANY)
HBM = pl.BlockSpec(memory_space=pltpu.HBM)
SMEM = pl.BlockSpec(memory_space=pltpu.SMEM)
VMEM = pl.BlockSpec(memory_space=pltpu.VMEM)


def table_kernel(
    me_ref,
    input_ref,
    target_ref,
    enc_ref,
    dec_ref,
    task_ref,
    k_ref,
    v_ref,
    *refs,
):
    kv_ref, table_ref, count_ref, held, sem = refs[-5:]
    me = me_ref[0]
    core = lax.rem(me, 2)
    half = held.shape[-1]
    columns = pl.ds(pl.multiple_of((1 - core) * half, half), half)
    into = [
        pltpu.make_async_copy(source.at[:, columns], held.at[tensor], sem.at[tensor])
        for tensor, source in enumerate((k_ref, v_ref))
    ]
    out = [
        pltpu.make_async_copy(held.at[tensor], kv_ref.at[tensor], sem.at[2 + tensor])
        for tensor in range(2)
    ]
    for copy in into:
        copy.start()
    total = enc_ref.shape[1]
    for side in range(2):
        pack = me + side * (1 - 2 * core)

        def find(item, carry, pack=pack):
            first, second = carry
            hit = enc_ref[0, item] == pack
            return (
                jnp.where(hit & (first < 0), item, first),
                jnp.where(hit & (first >= 0), item, second),
            )

        first, second = lax.fori_loop(0, total, find, (jnp.int32(-1), jnp.int32(-1)))
        second = jnp.maximum(second, 0)
        first = jnp.maximum(first, 0)
        for place, item in enumerate((first, second)):
            row = 2 * side + place
            dec = dec_ref[0, item]

            def before(other, offset, dec=dec):
                return offset + jnp.where(dec_ref[0, other] == dec, target_ref[0, other], 0)

            table_ref[row, 0] = dec ^ me
            table_ref[row, 1] = lax.fori_loop(0, item, before, jnp.int32(0))
            table_ref[row, 2] = target_ref[0, item]
            table_ref[row, 3] = jnp.int32(0) if place == 0 else input_ref[0, first]
            table_ref[row, 4] = input_ref[0, item]
            table_ref[row, 5] = task_ref[0, item]
            table_ref[row, 6] = 0
            table_ref[row, 7] = 0
    lane = lax.broadcasted_iota(jnp.int32, (1, 128), 1)
    counts = jnp.zeros((1, 128), jnp.float32)
    for item in range(total):
        amount = target_ref[0, item].astype(jnp.float32)
        counts = counts + jnp.where(lane == task_ref[0, item], amount, 0.0)
    count_ref[...] = counts
    for tensor in range(2):
        into[tensor].wait()
        out[tensor].start()
    for tensor in range(2):
        out[tensor].wait()


def tabulate(me, lengths, targets, enc_pack, dec_pack, task, keys, values):
    rows, features = keys.shape
    half = features // 2
    return pl.pallas_call(
        table_kernel,
        out_shape=[
            jax.ShapeDtypeStruct((2, rows, half), keys.dtype),
            jax.ShapeDtypeStruct((4, FIELDS), jnp.int32),
            jax.ShapeDtypeStruct((1, 128), jnp.float32),
        ],
        in_specs=[SMEM] * 6 + [HBM] * 2,
        out_specs=[ANY, SMEM, VMEM],
        scratch_shapes=[pltpu.VMEM((2, rows, half), keys.dtype), pltpu.SemaphoreType.DMA((4,))],
        compiler_params=ROOM,
        cost_estimate=SMALL,
        name="tabulate",
    )(me, lengths, targets, enc_pack, dec_pack, task, keys, values)


def split_kernel(me_ref, q_ref, c_ref, own_ref, other_ref, held, sem):
    half = held.shape[-1]
    core = lax.rem(me_ref[0], 2)
    into, out = [], []
    for side, (base, target) in enumerate(((core, own_ref), (1 - core, other_ref))):
        columns = pl.ds(pl.multiple_of(base * half, PAIR), half)
        for tensor, source in enumerate((q_ref, c_ref)):
            place = 2 * side + tensor
            into.append(
                pltpu.make_async_copy(source.at[:, columns], held.at[place], sem.at[place])
            )
            out.append(
                pltpu.make_async_copy(held.at[place], target.at[tensor], sem.at[4 + place])
            )
    for copy in into:
        copy.start()
    for place in range(4):
        into[place].wait()
        out[place].start()
    for copy in out:
        copy.wait()


def split(me, queries, cotangent):
    rows, features = queries.shape
    half = features // 2
    return pl.pallas_call(
        split_kernel,
        out_shape=[jax.ShapeDtypeStruct((2, rows, half), queries.dtype)] * 2,
        in_specs=[SMEM] + [HBM] * 2,
        out_specs=[ANY] * 2,
        scratch_shapes=[
            pltpu.VMEM((4, rows, half), queries.dtype),
            pltpu.SemaphoreType.DMA((8,)),
        ],
        compiler_params=ALONE,
        cost_estimate=SMALL,
        name="split_columns",
    )(me, queries, cotangent)


def attention_kernel(
    me_ref, table_ref, scale_ref, *refs, packs, first, bases, half, at
):
    pieces = refs[:packs]
    k_ref, v_ref, sibling_ref = refs[packs : packs + 3]
    outs = refs[packs + 3 + (0 if first else 3) :]
    k_out, v_out, sibling_out = outs[:3]
    query_outs = outs[3 : 2 + packs]
    loss_out = outs[2 + packs]
    kv, qc, dq, dkv, loss, scaling, in_sem, qc_sem, out_sem, dkv_sem = outs[packs + 3 :]
    width = qc.shape[-1]
    rows = qc.shape[2]
    keys = kv.shape[2]
    core = lax.rem(me_ref[0], 2)
    own_columns = pl.ds(pl.multiple_of(core * half + at, PAIR), width)
    half_columns = pl.ds(at, width)
    kv_copies = [
        [
            pltpu.make_async_copy(k_ref.at[:, own_columns], kv.at[0, 0], in_sem.at[0, 0]),
            pltpu.make_async_copy(v_ref.at[:, own_columns], kv.at[0, 1], in_sem.at[0, 1]),
        ],
        [
            pltpu.make_async_copy(
                sibling_ref.at[tensor, :, half_columns], kv.at[1, tensor], in_sem.at[1, tensor]
            )
            for tensor in range(2)
        ],
    ]
    dkv_copies = [
        [
            pltpu.make_async_copy(dkv.at[0, 0], k_out.at[:, own_columns], dkv_sem.at[0, 0]),
            pltpu.make_async_copy(dkv.at[0, 1], v_out.at[:, own_columns], dkv_sem.at[0, 1]),
        ],
        [
            pltpu.make_async_copy(
                dkv.at[1, tensor],
                sibling_out.at[pl.ds(tensor * keys, keys), half_columns],
                dkv_sem.at[1, tensor],
            )
            for tensor in range(2)
        ],
    ]
    for side in range(2):
        for copy in kv_copies[side]:
            copy.start()
        for place in range(2):
            item = 2 * side + place
            owner = table_ref[item, 0]
            for distance, piece in enumerate(pieces):

                @pl.when(owner == distance)
                def _(piece=piece, item=item, distance=distance):
                    pltpu.make_async_copy(
                        piece.at[:, :, pl.ds(at - bases[distance], width)],
                        qc.at[item],
                        qc_sem.at[item],
                    ).start()

    dq[...] = jnp.zeros_like(dq)
    loss[...] = jnp.zeros_like(loss)
    lane = lax.broadcasted_iota(jnp.int32, (1, PAIR), 1)
    low = lane < HEAD_DIM
    row = lax.broadcasted_iota(jnp.int32, (rows, PAIR), 0)
    row_lane = lax.broadcasted_iota(jnp.int32, (1, rows), 1)
    key = lax.broadcasted_iota(jnp.int32, (keys, 1), 0)
    key_lane = lax.broadcasted_iota(jnp.int32, (1, keys), 1)

    def dot(left, right):
        return jnp.dot(left, right, preferred_element_type=jnp.float32)

    vector = jnp.zeros((1, 128), jnp.float32)
    for side in range(2):
        for copy in kv_copies[side]:
            copy.wait()
        for place in range(2):
            item = 2 * side + place
            pltpu.make_async_copy(
                pieces[0].at[:, :, half_columns], qc.at[item], qc_sem.at[item]
            ).wait()
        owner, scale_rows = [], []
        border = table_ref[2 * side, 4]
        for place in range(2):
            item = 2 * side + place
            start, length = table_ref[item, 1], table_ref[item, 2]
            scale = scale_ref[0, table_ref[item, 5]]
            scaling[place] = jnp.where((row >= start) & (row < start + length), scale, 0.0)
            scale_rows.append(
                jnp.where((row_lane >= start) & (row_lane < start + length), scale, 0.0)
            )
            owner.append(table_ref[item, 0])

        def pair_chain(pair, side=side, owner=owner, scale_rows=scale_rows, border=border):
            columns = pl.ds(pl.multiple_of(pair * PAIR, PAIR), PAIR)
            early, early_lane = key < border, key_lane < border
            key_pair = kv[side, 0, :, columns]
            value_pair = kv[side, 1, :, columns]
            zero = jnp.zeros_like(key_pair)
            blank = jnp.zeros((HEAD_DIM, rows), key_pair.dtype)

            def by_example(array):
                return jnp.concatenate(
                    [jnp.where(early, array, zero), jnp.where(early, zero, array)], axis=1
                )

            def by_head(array):
                nothing = jnp.zeros_like(array)
                return jnp.concatenate(
                    [jnp.where(low, array, nothing), jnp.where(low, nothing, array)], axis=0
                )

            def spread(turned):
                blocks = []
                for array in turned:
                    blocks.append(jnp.concatenate([array[:HEAD_DIM], blank], axis=1))
                    blocks.append(jnp.concatenate([blank, array[HEAD_DIM:]], axis=1))
                return jnp.concatenate(blocks, axis=0)

            def example_parts(turned, part):
                array = turned[part]
                nothing = jnp.zeros_like(array)
                return jnp.concatenate(
                    [jnp.where(early_lane, array, nothing), jnp.where(early_lane, nothing, array)],
                    axis=0,
                )

            queries = [qc[2 * side + place, 0, :, columns] for place in range(2)]
            cots = [qc[2 * side + place, 1, :, columns] for place in range(2)]
            yield
            ups = [
                (cots[place].astype(jnp.float32) * scaling[place]).astype(jnp.bfloat16)
                for place in range(2)
            ]
            key_turned, value_turned = key_pair.T, value_pair.T
            cots_turned = [cot.T.astype(jnp.float32) for cot in cots]
            ups_turned = [
                (cots_turned[place] * scale_rows[place]).astype(jnp.bfloat16) for place in range(2)
            ]
            queries_turned = [query.T for query in queries]
            yield
            scores = dot(by_example(key_pair), spread(queries_turned))
            slopes = dot(by_example(value_pair), spread(ups_turned))
            yield
            lowest = jnp.float32(-3e38)
            highest = [
                jnp.max(jnp.where(early, scores, lowest), axis=0, keepdims=True),
                jnp.max(jnp.where(early, lowest, scores), axis=0, keepdims=True),
            ]
            yield
            powers = jnp.exp(scores - jnp.where(early, highest[0], highest[1]))
            inverse = [
                1.0 / jnp.sum(jnp.where(early, powers, 0.0), axis=0, keepdims=True),
                1.0 / jnp.sum(jnp.where(early, 0.0, powers), axis=0, keepdims=True),
            ]
            yield
            weights = powers * jnp.where(early, inverse[0], inverse[1])
            weights_low = weights.astype(jnp.bfloat16)
            yield
            drifts = [[], []]
            losses = []
            for head in range(2):
                part = slice(head * HEAD_DIM, (head + 1) * HEAD_DIM)
                lanes = slice(head * rows, (head + 1) * rows)
                attended = dot(example_parts(value_turned, part), weights_low[:, lanes])
                attended = attended.astype(jnp.bfloat16).astype(jnp.float32)
                for place in range(2):
                    item = 2 * side + place
                    here = attended[place * HEAD_DIM : (place + 1) * HEAD_DIM]
                    token = cots_turned[place][part] * here
                    losses.append(
                        (item, jnp.sum(token.reshape(HEAD_DIM // 8, 8, rows), axis=0))
                    )
                    drifts[place].append(
                        jnp.sum(
                            ups_turned[place][part].astype(jnp.float32) * here,
                            axis=0,
                            keepdims=True,
                        )
                    )
            yield
            drift = [jnp.concatenate(parts, axis=1) for parts in drifts]
            grad = weights * (slopes - jnp.where(early, drift[0], drift[1]))
            grad = grad.astype(jnp.bfloat16)
            yield
            query_parts = [[], []]
            for head in range(2):
                part = slice(head * HEAD_DIM, (head + 1) * HEAD_DIM)
                lanes = slice(head * rows, (head + 1) * rows)
                found = dot(example_parts(key_turned, part), grad[:, lanes])
                for place in range(2):
                    query_parts[place].append(found[place * HEAD_DIM : (place + 1) * HEAD_DIM])
            key_grad = dot(grad, jnp.concatenate([by_head(query) for query in queries], axis=1))
            value_grad = dot(weights_low, jnp.concatenate([by_head(up) for up in ups], axis=1))
            yield
            query_grads = [
                jnp.concatenate(query_parts[place], axis=0).astype(jnp.bfloat16).T
                for place in range(2)
            ]
            pair_grads = [
                jnp.where(early, found[:, :PAIR], found[:, PAIR:]).astype(jnp.bfloat16)
                for found in (key_grad, value_grad)
            ]
            yield
            for place in range(2):
                at = owner[place]
                dq[at, :, columns] = dq[at, :, columns] + query_grads[place]
            for tensor in range(2):
                dkv[side, tensor, :, columns] = pair_grads[tensor]
            for item, part in losses:
                loss[item] += part

        def group_step(group, carry, pair_chain=pair_chain):
            chains = [pair_chain(group * lockstep + i) for i in range(lockstep)]
            for _ in itertools.zip_longest(*chains):
                pass
            return carry

        lockstep = math.gcd(LOCKSTEP, width // PAIR)
        lax.fori_loop(0, width // PAIR // lockstep, group_step, 0)
        for copy in dkv_copies[side]:
            copy.start()
        for place in range(2):
            item = 2 * side + place
            start, length = table_ref[item, 1], table_ref[item, 2]
            part = jnp.sum(loss[item], axis=0, keepdims=True)
            part = jnp.where((row_lane >= start) & (row_lane < start + length), part, 0.0)
            amount = jnp.sum(part, axis=1, keepdims=True)
            vector = vector + jnp.where(lane == table_ref[item, 5], amount, 0.0)

    targets = [query_outs[0], sibling_out.at[pl.ds(2 * keys, rows), half_columns], *query_outs[1:]]
    query_copies = [
        pltpu.make_async_copy(dq.at[distance], target, out_sem.at[distance])
        for distance, target in enumerate(targets)
    ]
    for copy in query_copies:
        copy.start()
    loss_out[...] = vector
    for side in range(2):
        for copy in dkv_copies[side]:
            copy.wait()
    for copy in query_copies:
        copy.wait()


def attention_chunk(
    me, table, scales, pieces, keys, values, sibling, full, packs, bases, at, width
):
    rows = pieces[0].shape[1]
    key_rows, features = keys.shape
    half = features // 2
    low = jnp.bfloat16
    first = full is None
    flops = rows * key_rows * width
    before = 3 + packs + 3
    return pl.pallas_call(
        functools.partial(
            attention_kernel,
            packs=packs,
            first=first,
            bases=bases,
            half=half,
            at=at,
        ),
        out_shape=[
            jax.ShapeDtypeStruct(keys.shape, low),
            jax.ShapeDtypeStruct(keys.shape, low),
            jax.ShapeDtypeStruct((2 * key_rows + rows, half), low),
        ]
        + [jax.ShapeDtypeStruct((rows, width), low)] * (packs - 1)
        + [jax.ShapeDtypeStruct((1, 128), jnp.float32)],
        in_specs=[SMEM] * 3 + [ANY] * packs + [HBM] * 2 + [ANY] + [HBM] * (0 if first else 3),
        out_specs=[HBM] * 3 + [ANY] * (packs - 1) + [VMEM],
        scratch_shapes=[
            pltpu.VMEM((2, 2, key_rows, width), low),
            pltpu.VMEM((4, 2, rows, width), low),
            pltpu.VMEM((packs, rows, width), low),
            pltpu.VMEM((2, 2, key_rows, width), low),
            pltpu.VMEM((4, 8, rows), jnp.float32),
            pltpu.VMEM((2, rows, PAIR), jnp.float32),
            pltpu.SemaphoreType.DMA((2, 2)),
            pltpu.SemaphoreType.DMA((4,)),
            pltpu.SemaphoreType.DMA((packs,)),
            pltpu.SemaphoreType.DMA((2, 2)),
        ],
        input_output_aliases={} if first else {before + i: i for i in range(3)},
        compiler_params=pltpu.CompilerParams(
            vmem_limit_bytes=14 * 1024 * 1024 + 2 * packs * rows * width
        ),
        cost_estimate=pl.CostEstimate(
            flops=flops, bytes_accessed=8 * 1024 * 1024, transcendentals=0
        ),
        name="attention_chunk",
    )(me, table, scales, *pieces, keys, values, sibling, *(() if first else full))


def finish_kernel(me_ref, *refs, counts, starts, half):
    back = refs[sum(counts)]
    outs = refs[sum(counts) + 3 : sum(counts) + 6]
    *merged, sem = refs[sum(counts) + 6 :]
    rows, keys = merged[0].shape[1], outs[1].shape[0]
    core = lax.rem(me_ref[0], 2)
    copies = []

    def write(source, out, columns):
        copies.append(pltpu.make_async_copy(source, out.at[:, columns], sem.at[len(copies)]))
        copies[-1].start()

    other = pl.ds(pl.multiple_of((1 - core) * half, PAIR), half)
    for tensor in range(2):
        write(back.at[pl.ds(tensor * keys, keys)], outs[1 + tensor], other)
    given = list(refs[: sum(counts)])
    for chunk, (at, held) in enumerate(zip(starts, merged)):
        width = held.shape[-1]
        for side, base in enumerate((core, 1 - core)):
            terms = [given.pop(0)[...] for _ in range(counts[2 * chunk + side])]
            if side == 1:
                terms.append(back[2 * keys : 2 * keys + rows, at : at + width])
            held[side] = functools.reduce(jnp.add, terms)
            columns = pl.ds(pl.multiple_of(base * half + at, PAIR), width)
            write(held.at[side], outs[0], columns)
    for copy in copies:
        copy.wait()


def finish(me, ends, starts, packs, back, like, keys, values):
    parts = [part for near, far in ends for part in near + far]
    counts = [len(side) for end in ends for side in end]
    return pl.pallas_call(
        functools.partial(
            finish_kernel, counts=counts, starts=starts, half=like.shape[1] // 2
        ),
        out_shape=[
            jax.ShapeDtypeStruct(array.shape, array.dtype) for array in (like, keys, values)
        ],
        in_specs=[SMEM] + [VMEM] * (len(parts) + 1) + [HBM] * 2,
        out_specs=[HBM] * 3,
        scratch_shapes=[pltpu.VMEM((2, *near[0].shape), like.dtype) for near, _ in ends]
        + [pltpu.SemaphoreType.DMA((2 + 2 * len(ends),))],
        input_output_aliases={len(parts) + 2: 1, len(parts) + 3: 2},
        compiler_params=pltpu.CompilerParams(vmem_limit_bytes=(8 + packs) * 1024 * 1024),
        cost_estimate=SMALL,
        name="finish",
    )(me, *parts, back, keys, values)


def swap(array, axis_name, size, bits):
    return lax.ppermute(array, axis_name, [(i, i ^ bits) for i in range(size)])


def doubled_sum(array, axis_name, size, first=1, last=None):
    step = first
    while step < (last or size):
        array = array + swap(array, axis_name, size, step)
        step *= 2
    return array


together = lax.optimization_barrier


def local(
    enc_keys,
    enc_values,
    dec_queries,
    cotangent,
    input_lengths,
    target_lengths,
    enc_pack,
    dec_pack,
    task_group,
    dro_weights,
    *,
    packs,
    groups,
):
    me = lax.axis_index("pack").astype(jnp.int32).reshape(1)
    rows, features = dec_queries.shape
    half = features // 2
    total_tokens = rows * packs * groups
    relayed = packs == 8

    def swapped(array, bits):
        return swap(array, "pack", packs, bits)

    def tabulated(me):
        return tabulate(
            me,
            input_lengths,
            target_lengths,
            enc_pack,
            dec_pack,
            task_group[:, :, 0],
            enc_keys,
            enc_values,
        )

    def scales_of(group_counts):
        counts = doubled_sum(group_counts, "dp", groups)
        weights = dro_weights.astype(jnp.float32)
        weights = jnp.pad(weights, (0, 128 - GROUPS)).reshape(1, 128)
        return counts, weights / jnp.sum(weights) * (total_tokens / counts)

    widths = [half * share // sum(CHUNKS) for share in CHUNKS]
    starts = [sum(widths[:i]) for i in range(len(widths))]
    spots = list(zip(starts, widths))
    own, other = split(me, dec_queries, cotangent)
    if not relayed:
        pieces = [own] + [swapped(other if i & 1 else own, i) for i in range(1, packs)]
        kv_other, table, group_counts = tabulated(me)
        kv_sibling = swapped(kv_other, 1)
        counts, scales = scales_of(group_counts)
        full, losses, ends = None, [], []
        for at, width in spots:
            *result, loss = attention_chunk(
                me, table, scales, pieces, enc_keys, enc_values, kv_sibling, full,
                packs, [0] * packs, at, width,
            )
            full, parts = result[:3], result[3:]
            losses.append(loss)
            arrived = [swapped(part, i) for i, part in enumerate(parts[1:], 2)]
            ends.append((parts[:1] + arrived[0::2], arrived[1::2]))
        back = swapped(full[2], 1)
        loss = doubled_sum(functools.reduce(jnp.add, losses), "pack", packs)
        loss = doubled_sum(loss, "dp", groups)
    else:
        first = widths[0]
        x_own, y_own = swapped(own, 2), swapped(own, 4)
        x_other, y_other = swapped(other, 3), swapped(other, 5)
        sibling = swapped(other, 1)
        me_later, x_own = together((me, x_own))
        kv_other, table, group_counts = tabulated(me_later)
        near = [x_own[:, :, :first], x_own[:, :, first:]]
        x_own, y_own, x_other, y_other, sibling, kv_other, group_counts, table, near = together(
            (x_own, y_own, x_other, y_other, sibling, kv_other, group_counts, table, near)
        )
        far = [y_other[:, :, :first], y_other[:, :, first:]]
        diagonal = [swapped(near[0], 4), swapped(far[0], 2)]
        kv_sibling = swapped(kv_other, 1)
        counts, scales = scales_of(group_counts)
        diagonal, near, far, kv_sibling, scales = together(
            (diagonal, near, far, kv_sibling, scales)
        )
        later = [swapped(near[1], 4), swapped(far[1], 2)]

        def attend(full, chunk, diagonal, base):
            at, width = spots[chunk]
            pieces = [own, sibling, x_own, x_other, y_own, y_other, *diagonal]
            *result, loss = attention_chunk(
                me, table, scales, pieces, enc_keys, enc_values, kv_sibling, full,
                packs, [0] * 6 + [base] * 2, at, width,
            )
            return result[:3], result[3:], loss

        def forwarded(parts):
            return [swapped(parts[5], 2), swapped(parts[6], 4)]

        def sent(parts):
            return [swapped(parts[1], 2), swapped(parts[4], 5)]

        def merged(parts, relay):
            return [swapped(parts[3] + relay[0], 4), swapped(parts[2] + relay[1], 3)]

        def sums(parts, direct, last):
            return [parts[0], direct[0], last[0]], [direct[1], last[1]]

        full, parts_a, loss_a = attend(None, 0, diagonal, 0)
        later, full, parts_a = together((later, full, parts_a))

        relay_a, direct_a = forwarded(parts_a), sent(parts_a)
        full, parts_b, loss_b = attend(full, 1, later, first)
        relay_a, direct_a, full, parts_b, loss_b = together(
            (relay_a, direct_a, full, parts_b, loss_b)
        )

        last_a, relay_b = merged(parts_a, relay_a), forwarded(parts_b)
        loss = doubled_sum(loss_a + loss_b, "dp", groups)
        loss = doubled_sum(loss, "pack", packs, 2, 4)
        last_a, relay_b, loss, full = together((last_a, relay_b, loss, full))

        last_b, direct_b = merged(parts_b, relay_b), sent(parts_b)
        back = swapped(full[2], 1)
        loss = doubled_sum(loss, "pack", packs, 4)
        last_b, direct_b, back, loss = together((last_b, direct_b, back, loss))
        loss = doubled_sum(loss, "pack", packs, 1, 2)
        ends = [sums(parts_a, direct_a, last_a), sums(parts_b, direct_b, last_b)]

    queries_gradient, keys_gradient, values_gradient = finish(
        me, ends, starts, packs, back, dec_queries, *full[:2]
    )
    group_loss = (loss / counts)[0, :GROUPS]
    return (queries_gradient, keys_gradient, values_gradient, group_loss)


def solution(mesh):
    placed = (
        P(("dp", "pack"), None),
        P(("dp", "pack"), None),
        P(("dp", "pack"), None),
        P(("dp", "pack"), None),
        P("dp", None),
        P("dp", None),
        P("dp", None),
        P("dp", None),
        P("dp", None, None),
        P(),
    )
    return jax.shard_map(
        functools.partial(local, packs=mesh.shape["pack"], groups=mesh.shape["dp"]),
        mesh=mesh,
        in_specs=placed,
        out_specs=(P(("dp", "pack"), None), P(("dp", "pack"), None), P(("dp", "pack"), None), P()),
        check_vma=False,
    )
```
